128 devices in a mesh: mlong: 16 (over z_lo, y, core), mshort: 8 (over z_hi, x).
Axes of the slice: x: 4, y: 4, z: 4 (z_hi: 2, z_lo: 2; z = z_hi * 2 + z_lo), core: 2. Of those that a mesh axis runs over, the one named last changes fastest.
Arguments:
- acq_traces: bfloat16 [65536, 1024], P(('mlong', 'mshort')), may hold values from -6 to 6
- route_owner: int32 [65536], P(('mlong', 'mshort')), may hold values from -1 to 127, as said below
- route_row: int32 [65536], P(('mlong', 'mshort')), may hold values from -1 to 511, as said below
- route_fold: int32 [65536], P(('mlong', 'mshort')), may hold values from 0 to 3
- sample_bits: int32 [65536, 64], P(('mlong', 'mshort')), may hold values from 0 to 65535
- left_factors: bfloat16 [65536, 4, 128], P(('mlong', 'mshort')), may hold values from -0.5 to 0.5
- right_factors: bfloat16 [4, 131072, 128], P(None, ('mlong', 'mshort')), may hold values from -6 to 6
Outputs:
- new_right: float32 [4, 131072, 128], P(None, ('mlong', 'mshort'))
- trace_residuals: bfloat16 [65536, 1024], P(('mlong', 'mshort'))
The draws below stay inside these ranges and needn't reach their ends.
Inputs may be any that keep to these rules, and one draw needn't show every extreme that they name: route_owner: -1 marks an empty slot. In each device's 16 * 32 slots no owner is named more than 4 times; some owner is named exactly 4 times in every device's slots. Every owner is named somewhere. route_row: -1 exactly where route_owner is -1. No pair (route_owner, route_row) occurs twice.
All inputs are finite; a program needn't handle non-finite values.
Results may differ from the reference program's by a relative error of at most 0.0036.
Values may be sent and summed in bfloat16 or wider, within the bound.
No kernel may reach another device: no remote copies, remote signals or barrier semaphores. Data moves between devices by JAX's collectives and lax.ppermute only.
A program may use at most 64 MiB of HBM per device.

```python
import jax
import jax.numpy as jnp
from jax import lax

W = 1024
RANK = 128
FOLDS = 4
H = 4
CX = 16
CY = 32
NX = 256
NY = 256
NROWS = 65536
NCOLS = 131072
N_MLONG = 16
N_MSHORT = 8


def routing(key):
    rows = CX * CY
    peers = NROWS // rows
    cap = rows // peers
    keys = jax.random.split(key, 5)
    full_dest = jax.random.randint(keys[0], (), 0, peers)
    hot = jax.random.randint(keys[1], (peers,), 1, 2 * cap + 1)
    raw = jax.random.randint(keys[2], (peers, peers), 0, 2 * cap + 1)
    count = jnp.minimum(jnp.minimum(raw, hot[None, :]), cap - 1)
    count = jnp.maximum(count, jnp.eye(peers, dtype=jnp.int32))
    dest = jnp.arange(peers, dtype=jnp.int32)
    count = jnp.where(dest[None, :] == full_dest, cap, count)
    offset = jnp.cumsum(count, axis=0) - count
    perms = jax.vmap(lambda k: jax.random.permutation(k, rows))(jax.random.split(keys[3], peers)).astype(jnp.int32)
    slot = jnp.arange(cap, dtype=jnp.int32)
    live = slot[None, None, :] < count[:, :, None]
    index = jnp.minimum(offset[:, :, None] + slot[None, None, :], rows - 1)
    chosen = perms[jnp.broadcast_to(dest[None, :, None], index.shape), index]
    owner = jnp.where(live, jnp.broadcast_to(dest[None, :, None], index.shape), -1).reshape(peers, rows)
    local = jnp.where(live, chosen, -1).reshape(peers, rows)
    order = jax.vmap(lambda k: jax.random.permutation(k, rows))(jax.random.split(keys[4], peers)).astype(jnp.int32)
    owner = jnp.take_along_axis(owner, order, axis=1)
    local = jnp.take_along_axis(local, order, axis=1)
    return (owner.reshape(-1).astype(jnp.int32), local.reshape(-1).astype(jnp.int32))


def draw_route_owner(key, part):
    return routing(key)[0]


def draw_route_row(key, part):
    return routing(key)[1]


def plant(values, key, low, largest):
    longest = values.shape.index(max(values.shape))
    spots = []
    for shift in (0, 1):
        where = [jax.random.randint(jax.random.fold_in(key, axis), (), 0, length) for axis, length in enumerate(values.shape)]
        where[longest] = (where[longest] + shift) % values.shape[longest]
        spots.append(tuple(where))
    return values.at[spots[0]].set(low).at[spots[1]].set(largest)


def block_levels(stream_key, extent, pieces, least, high):
    factor_of = 1.0
    for axis_at, shards_of in pieces:
        heights = jax.random.uniform(jax.random.fold_in(jax.random.fold_in(stream_key, 6), axis_at), (shards_of,), jnp.float32, least / len(pieces), high / len(pieces))
        factor_of = factor_of * jnp.repeat(jnp.exp(heights), extent[axis_at] // shards_of).reshape((-1,) + (1,) * (len(extent) - 1 - axis_at))
    return factor_of


def normal_values(rng, shape, width, bound, cuts=(), kind=jnp.bfloat16):
    factor_of = block_levels(rng, shape, cuts, -0.22, 0.18) if cuts else 1.0
    values = jax.random.normal(rng, shape, jnp.float32) * width * factor_of
    return jnp.minimum(jnp.maximum(values, -bound), bound).astype(kind)


def setup_inputs(seed: int = 0) -> dict:
    key_list = jax.random.split(jax.random.key(seed), 8)
    acq_traces = normal_values(key_list[0], (NROWS, W), 1.0, 6.0, ((0, 128),))
    route_owner = draw_route_owner(jax.random.fold_in(key_list[7], 71), 0)
    route_row = draw_route_row(jax.random.fold_in(key_list[7], 71), 0)
    route_fold = plant(jax.random.randint(key_list[3], (NROWS,), 0, FOLDS), jax.random.fold_in(key_list[3], 1), 0, FOLDS - 1).astype(jnp.int32)
    sample_bits = plant(jax.random.randint(key_list[4], (NROWS, W // 16), 0, 65536), jax.random.fold_in(key_list[4], 1), 0, 65535).astype(jnp.int32)
    left_factors = normal_values(key_list[5], (NROWS, FOLDS, RANK), RANK ** -0.5, 0.5, ((0, 128),))
    right_factors = normal_values(key_list[6], (FOLDS, NCOLS, RANK), 1.0, 6.0, ((1, 128),))
    return {"acq_traces": acq_traces, "route_owner": route_owner, "route_row": route_row, "route_fold": route_fold, "sample_bits": sample_bits, "left_factors": left_factors, "right_factors": right_factors}


def unpack(bits):
    shifts = jnp.arange(16, dtype=jnp.int32)
    flags = jnp.bitwise_and(lax.shift_right_logical(bits[:, :, None], shifts[None, None, :]), 1)
    return flags.reshape(bits.shape[0], -1).astype(jnp.float32)

def chol_right(cross, gram):
    chol = jnp.linalg.cholesky(gram)
    first = lax.linalg.triangular_solve(chol, cross, left_side=False, lower=True, transpose_a=True)
    return lax.linalg.triangular_solve(chol, first, left_side=False, lower=True, transpose_a=False)

def to_grid(values):
    tail = values.shape[1:]
    values = values.reshape((N_MLONG, N_MSHORT, CX, CY) + tail)
    values = jnp.moveaxis(values, 2, 1)
    return values.reshape((NX, NY) + tail)

def reference(acq_traces, route_owner, route_row, route_fold, sample_bits, left_factors, right_factors):
    rows = CX * CY
    peers = N_MLONG * N_MSHORT
    valid = route_owner >= 0
    target = jnp.where(valid, route_owner * rows + route_row, NROWS).astype(jnp.int32)
    data = jnp.zeros((NROWS, W), jnp.bfloat16).at[target].set(acq_traces, mode='drop')
    fold = jnp.full((NROWS,), -1, jnp.int32).at[target].set(route_fold, mode='drop')
    pad2 = ((H, H), (H, H))
    data_p = jnp.pad(to_grid(data), pad2 + ((0, 0),))
    bits_p = jnp.pad(to_grid(sample_bits), pad2 + ((0, 0),))
    fold_p = jnp.pad(to_grid(fold), pad2, constant_values=-1)
    left_p = jnp.pad(to_grid(left_factors), pad2 + ((0, 0), (0, 0)))
    ridge = jnp.eye(RANK, dtype=jnp.float32)
    wx = CX + 2 * H
    wy = CY + 2 * H

    def window(dev):
        xa = dev // N_MSHORT * CX
        yb = dev % N_MSHORT * CY
        zero = jnp.zeros((), jnp.int32)
        d_win = lax.dynamic_slice(data_p, (xa, yb, zero), (wx, wy, W))
        b_win = lax.dynamic_slice(bits_p, (xa, yb, zero), (wx, wy, W // 16))
        f_win = lax.dynamic_slice(fold_p, (xa, yb), (wx, wy))
        l_win = lax.dynamic_slice(left_p, (xa, yb, zero, zero), (wx, wy, FOLDS, RANK))
        v_win = lax.dynamic_slice(right_factors, (zero, dev * W, zero), (FOLDS, W, RANK))
        d_core = d_win[H:H + CX, H:H + CY].reshape(rows, W)
        f_core = f_win[H:H + CX, H:H + CY].reshape(rows)
        l_core = l_win[H:H + CX, H:H + CY].reshape(rows, FOLDS, RANK)
        s_core = unpack(b_win[H:H + CX, H:H + CY].reshape(rows, W // 16)) * (f_core >= 0)[:, None].astype(jnp.float32)
        d_win = d_win.reshape(-1, W)
        f_win = f_win.reshape(-1)
        l_win = l_win.reshape(-1, FOLDS, RANK)
        seen = unpack(b_win.reshape(-1, W // 16)) * (f_win >= 0)[:, None].astype(jnp.float32)
        news = []
        chosen = jnp.zeros((rows, W), jnp.float32)
        for f in range(FOLDS):
            lf = l_win[:, f]
            pred = jnp.dot(lf.astype(jnp.float32), v_win[f].T.astype(jnp.float32), preferred_element_type=jnp.float32)
            train = seen * (f_win != f)[:, None].astype(jnp.float32)
            filled = (train * d_win.astype(jnp.float32) + (1.0 - train) * pred).astype(jnp.bfloat16)
            cross = jnp.dot(filled.T.astype(jnp.float32), lf.astype(jnp.float32), preferred_element_type=jnp.float32)
            gram = jnp.dot(lf.T.astype(jnp.float32), lf.astype(jnp.float32), preferred_element_type=jnp.float32) + ridge
            newv = chol_right(cross, gram)
            news.append(newv)
            core_pred = jnp.dot(l_core[:, f].astype(jnp.float32), newv.astype(jnp.bfloat16).T.astype(jnp.float32), preferred_element_type=jnp.float32)
            chosen = chosen + (f_core == f)[:, None].astype(jnp.float32) * core_pred
        resid = (s_core * (d_core.astype(jnp.float32) - chosen)).astype(jnp.bfloat16)
        return (jnp.stack(news), resid)
    news, resid = lax.map(window, jnp.arange(peers, dtype=jnp.int32))
    new_right = jnp.moveaxis(news, 0, 1).reshape(FOLDS, NCOLS, RANK)
    resid = resid.reshape(NROWS, W)
    picked = jnp.take(resid, jnp.minimum(target, NROWS - 1), axis=0)
    trace_residuals = jnp.where(valid[:, None], picked, jnp.zeros((), jnp.bfloat16))
    return (new_right, trace_residuals)
```

```python
import jax
import jax.numpy as jnp
from jax import lax
from jax.experimental import pallas as pl
from jax.experimental.pallas import tpu as pltpu
from jax.sharding import PartitionSpec as P

RANK = 128
FOLDS = 4
H = 4
CX = 16
CY = 32
W = 1024
ROWS = CX * CY
HALF = W // 2
LANE = 128
CAP = 4
SLOT = 2 * CAP
NSLOT = 128 * SLOT
EXT = W + LANE
LEXT = FOLDS * RANK + LANE
STRIP = H * CY
SIDE = H * CX
TALL = H * (CX + 2 * H)
HALO = 2 * STRIP + 2 * TALL
PANEL = 16

BF = jnp.bfloat16
F32 = jnp.float32
AXES = ("mlong", "mshort")


def _iota(shape, dim):
    return lax.broadcasted_iota(jnp.int32, shape, dim)


def _hot(cond):
    return jnp.where(cond, 1.0, 0.0).astype(BF)


def _dot(a, b):
    return jnp.dot(a, b, preferred_element_type=F32)


def _dot_nt(a, b):
    return lax.dot_general(a, b, (((1,), (1,)), ((), ())), preferred_element_type=F32)


def _params(limit=32):
    return pltpu.CompilerParams(vmem_limit_bytes=limit * 1024 * 1024)


def _cost(flops, nbytes):
    return pl.CostEstimate(flops=flops, bytes_accessed=nbytes, transcendentals=0)


def _side_select(shape, first):
    r = _iota(shape, 0)
    m = _iota(shape, 1)
    return _hot(m == (r // H) * CY + first + r % H)


def _route_body(own_ref, row_ref, fold_ref, tr_ref, send_ref, place_ref):
    own = own_ref[...]
    row = row_ref[...]
    valid = own >= 0
    ownf = own.astype(F32)
    sub = _iota((LANE, ROWS), 0)
    flag = jnp.where(valid, 1.0, 0.0)
    meta = jnp.where(sub == 0, flag, 0.0)
    meta = jnp.where(sub == 1, (row >> 5).astype(F32), meta)
    meta = jnp.where(sub == 2, (row & 31).astype(F32), meta)
    meta = jnp.where(sub == 3, (fold_ref[...] + 1).astype(F32), meta)
    meta = jnp.where(sub == 4, ownf, meta)
    meta_t = meta.T
    ocol = meta_t[:, 4:5]
    same = ocol == ownf
    rs = _iota((ROWS, ROWS), 0)
    cs = _iota((ROWS, ROWS), 1)
    within = jnp.sum(jnp.where(same & (rs < cs), 1.0, 0.0), axis=0, keepdims=True)
    place = jnp.where(valid, ownf * SLOT + within, -64.0).astype(jnp.int32)
    within_c = jnp.sum(jnp.where(same & (cs < rs), 1.0, 0.0), axis=1, keepdims=True)
    place_c = jnp.where(ocol >= 0.0, ocol * SLOT + within_c, -64.0)
    place_ref[...] = jnp.broadcast_to(place_c, (ROWS, LANE)).astype(jnp.int32)
    meta_b = meta_t.astype(BF)
    step = 256
    for base in range(0, NSLOT, step):
        r = _iota((step, ROWS), 0) + base
        hot0 = _hot(r == place)
        hot1 = _hot(r == place + CAP)
        y = _dot(hot0, tr_ref[:, :HALF]) + _dot(hot1, tr_ref[:, HALF:])
        send_ref[base : base + step, :HALF] = y.astype(BF)
        send_ref[base : base + step, HALF:] = _dot(hot0 + hot1, meta_b).astype(BF)


def _route(own, row, fold, traces):
    return pl.pallas_call(
        _route_body,
        out_shape=(
            jax.ShapeDtypeStruct((NSLOT, HALF + LANE), BF),
            jax.ShapeDtypeStruct((ROWS, LANE), jnp.int32),
        ),
        compiler_params=_params(60),
        cost_estimate=_cost(10**9, 4 * 10**6),
        name="route",
    )(own, row, fold, traces)


def _slot_rows(meta):
    return jnp.where(meta[0] > 0.5, meta[1] * CY + meta[2], -1.0).astype(jnp.int32)


def _place_body(got_ref, core_ref, top_ref, bot_ref, left_ref, right_ref):
    meta = got_ref[:, HALF:].astype(F32).T
    m = _slot_rows((meta[0:1], meta[1:2], meta[2:3]))
    half = (_iota((1, NSLOT), 1) // CAP) % 2
    m0 = jnp.where(half == 0, m, -1)
    m1 = jnp.where(half == 1, m, -1)
    step = 128
    for base in range(0, ROWS, step):
        r = _iota((step, NSLOT), 0) + base
        hot0 = _hot(r == m0)
        hot1 = _hot(r == m1)
        d0 = _dot(hot0, got_ref[:, :HALF]).astype(BF)
        d1 = _dot(hot1, got_ref[:, :HALF]).astype(BF)
        f = _dot(hot0, got_ref[:, HALF:])[:, 3:4]
        f = jnp.broadcast_to(f, (step, LANE)).astype(BF)
        spots = [(core_ref, base)]
        if base == 0:
            spots.append((top_ref, 0))
        if base == ROWS - STRIP:
            spots.append((bot_ref, 0))
        for ref, at in spots:
            ref[at : at + step, :HALF] = d0
            ref[at : at + step, HALF:W] = d1
            ref[at : at + step, W:] = f
    core = core_ref[...]
    left_ref[...] = _dot(_side_select((SIDE, ROWS), 0), core).astype(BF)
    right_ref[...] = _dot(_side_select((SIDE, ROWS), CY - H), core).astype(BF)


def _place(got):
    return pl.pallas_call(
        _place_body,
        out_shape=(
            jax.ShapeDtypeStruct((ROWS, EXT), BF),
            jax.ShapeDtypeStruct((STRIP, EXT), BF),
            jax.ShapeDtypeStruct((STRIP, EXT), BF),
            jax.ShapeDtypeStruct((SIDE, EXT), BF),
            jax.ShapeDtypeStruct((SIDE, EXT), BF),
        ),
        compiler_params=_params(),
        cost_estimate=_cost(10**9, 4 * 10**6),
        name="to_grid",
    )(got)


def _pack_body(up_ref, down_ref, left_ref, right_ref, to_left_ref, to_right_ref):
    for first, side, out in ((0, left_ref, to_left_ref), (CY - H, right_ref, to_right_ref)):
        pick = _side_select((H * H, STRIP), first)
        out[: H * H, :] = _dot(pick, up_ref[...]).astype(BF)
        out[H * H : H * H + SIDE, :] = side[...]
        out[H * H + SIDE :, :] = _dot(pick, down_ref[...]).astype(BF)


def _pack(up, down, left, right, name):
    width = up.shape[1]
    return pl.pallas_call(
        _pack_body,
        out_shape=(
            jax.ShapeDtypeStruct((TALL, width), BF),
            jax.ShapeDtypeStruct((TALL, width), BF),
        ),
        compiler_params=_params(),
        cost_estimate=_cost(10**7, 10**6),
        name=name,
    )(up, down, left, right)


def _along(to_up, to_down, axis):
    fwd = [(i, i + 1) for i in range(lax.axis_size(axis) - 1)]
    before = lax.ppermute(to_down, axis, fwd)
    after = lax.ppermute(to_up, axis, [(j, i) for i, j in fwd])
    return before, after


def _lext_body(left_ref, bits_ref, core_ref, top_ref, bot_ref, lside_ref, rside_ref):
    core_ref[:, : FOLDS * RANK] = left_ref[...]
    bits = bits_ref[...]
    low = (bits & 255).astype(F32)
    high = (bits >> 8).astype(F32)
    core_ref[:, FOLDS * RANK :] = jnp.concatenate([low, high], axis=1).astype(BF)
    core = core_ref[...]
    top_ref[...] = core[:STRIP]
    bot_ref[...] = core[ROWS - STRIP :]
    lside_ref[...] = _dot(_side_select((SIDE, ROWS), 0), core).astype(BF)
    rside_ref[...] = _dot(_side_select((SIDE, ROWS), CY - H), core).astype(BF)


def _lext(left, bits):
    return pl.pallas_call(
        _lext_body,
        out_shape=(
            jax.ShapeDtypeStruct((ROWS, LEXT), BF),
            jax.ShapeDtypeStruct((STRIP, LEXT), BF),
            jax.ShapeDtypeStruct((STRIP, LEXT), BF),
            jax.ShapeDtypeStruct((SIDE, LEXT), BF),
            jax.ShapeDtypeStruct((SIDE, LEXT), BF),
        ),
        compiler_params=_params(),
        cost_estimate=_cost(10**8, 2 * 10**6),
        name="left_rows",
    )(left, bits)


def _recip(x):
    r = pl.reciprocal(x, approx=True)
    r = r * (2.0 - x * r)
    return r * (2.0 - x * r)


def _split3(x):
    hi = x.astype(BF)
    rest = x - hi.astype(F32)
    mid = rest.astype(BF)
    return hi, mid, (rest - mid.astype(F32)).astype(BF)


def _outer6(a, b):
    ah, am, al = _split3(a)
    bh, bm, bl = _split3(b)
    left = jnp.concatenate([ah, ah, am, ah, am, al], axis=0)
    right = jnp.concatenate([bh, bm, bh, bl, bm, bh], axis=0)
    return lax.dot_general(left, right, (((0,), (0,)), ((), ())), preferred_element_type=F32)


def _eliminate(g_ref, first, last):
    lane = _iota((FOLDS, PANEL, RANK), 2)
    sub = _iota((FOLDS, PANEL, RANK), 1)
    lane8 = _iota((FOLDS, 8, RANK), 2)
    lane_all = _iota((RANK, RANK), 1)
    rep = lambda a, n: jnp.broadcast_to(a, (FOLDS, n, RANK))
    tall = lambda a: jnp.concatenate([a] * (PANEL // 8), axis=1)
    for lo in range(first, last, PANEL):
        start = g_ref[:, lo : lo + PANEL, :]
        x = start
        for k in range(0, PANEL, 4):
            c = lo + k
            c0, c1, c2, c3 = (rep(x[:, :, c + j : c + j + 1], PANEL) for j in range(4))
            group8 = (lane8 >= c) & (lane8 < c + 4)
            r0, r1, r2, r3 = (
                jnp.where(group8, jnp.where(lane8 == c + i, 1.0, 0.0), rep(x[:, k + i : k + i + 1, :], 8)) for i in range(4)
            )
            at = lambda col, i: rep(col[:, k + i : k + i + 1, :], 8)
            p00, p01, p02, p03 = at(c0, 0), at(c1, 0), at(c2, 0), at(c3, 0)
            e0 = _recip(p00)
            l10, l20, l30 = p01 * e0, p02 * e0, p03 * e0
            e1 = _recip(at(c1, 1) - l10 * p01)
            p12, p13 = at(c2, 1) - l10 * p02, at(c3, 1) - l10 * p03
            l21, l31 = p12 * e1, p13 * e1
            e2 = _recip(at(c2, 2) - l20 * p02 - l21 * p12)
            p23 = at(c3, 2) - l20 * p03 - l21 * p13
            l32 = p23 * e2
            e3 = _recip(at(c3, 3) - l30 * p03 - l31 * p13 - l32 * p23)
            r1 = r1 - l10 * r0
            r2 = r2 - l20 * r0 - l21 * r1
            r3 = r3 - l30 * r0 - l31 * r1 - l32 * r2
            w0, w1, w2, w3 = e0 * r0, e1 * r1, e2 * r2, e3 * r3
            c1 = c1 - tall(l10) * c0
            c2 = c2 - tall(l20) * c0 - tall(l21) * c1
            c3 = c3 - tall(l30) * c0 - tall(l31) * c1 - tall(l32) * c2
            x = jnp.where((lane >= c) & (lane < c + 4), 0.0, x)
            x = x - c0 * tall(w0) - c1 * tall(w1) - c2 * tall(w2) - c3 * tall(w3)
            z2 = w2 - l32 * w3
            z1 = w1 - l21 * z2 - l31 * w3
            z0 = w0 - l10 * z1 - l20 * z2 - l30 * w3
            for i, z in enumerate((z0, z1, z2, w3)):
                x = jnp.where(sub == k + i, tall(z), x)
        signed = jnp.where(lane < lo, -start, start)
        inside = (lane_all >= lo) & (lane_all < lo + PANEL)
        for f in range(FOLDS):
            g_ref[f] = jnp.where(inside, 0.0, g_ref[f]) - _outer6(signed[f], x[f])
        g_ref[:, lo : lo + PANEL, :] = x


def _unpack(rows):
    b = _iota((LANE, W), 0)
    o = _iota((LANE, W), 1)
    spread = _hot(b == (o // 16) + jnp.where(o % 16 >= 8, 64, 0))
    value = _dot(rows, spread).astype(jnp.int32)
    shift = _iota(value.shape, 1) % 8
    return ((value >> shift) & 1).astype(F32).astype(BF)


def _core_prep_body(core_ref, ltc_ref, seen_ref, gram_ref):
    eye = jnp.where(_iota((RANK, RANK), 0) == _iota((RANK, RANK), 1), 1.0, 0.0)
    for f in range(FOLDS):
        core = core_ref[:, f * RANK : (f + 1) * RANK]
        core_t = core.T
        ltc_ref[f] = core_t
        gram_ref[f] = _dot(core_t, core) + eye
    for base in range(0, ROWS, 128):
        seen_ref[base : base + 128, :] = _unpack(core_ref[base : base + 128, FOLDS * RANK :])


def _core_prep(core):
    return pl.pallas_call(
        _core_prep_body,
        out_shape=(
            jax.ShapeDtypeStruct((FOLDS, RANK, ROWS), BF),
            jax.ShapeDtypeStruct((ROWS, W), BF),
            jax.ShapeDtypeStruct((FOLDS, RANK, RANK), F32),
        ),
        compiler_params=_params(),
        cost_estimate=_cost(10**9, 2 * 10**6),
        name="core_prep",
    )(core)


def _inverse_body(gram_ref, up_ref, down_ref, before_ref, after_ref, lth_ref, seen_ref, inv_ref):
    halos = (up_ref, down_ref, before_ref, after_ref)
    for f in range(FOLDS):
        halo = jnp.concatenate([r[:, f * RANK : (f + 1) * RANK] for r in halos], axis=0)
        halo_t = halo.T
        lth_ref[f] = halo_t
        inv_ref[f] = gram_ref[f] + _dot(halo_t, halo)
    at = 0
    for ref in halos:
        n = ref.shape[0]
        seen_ref[at : at + n, :] = _unpack(ref[:, FOLDS * RANK :])
        at += n
    _eliminate(inv_ref, 0, RANK)


def _inverse(gram, up, down, before, after):
    return pl.pallas_call(
        _inverse_body,
        out_shape=(
            jax.ShapeDtypeStruct((FOLDS, RANK, HALO), BF),
            jax.ShapeDtypeStruct((HALO, W), BF),
            jax.ShapeDtypeStruct((FOLDS, RANK, RANK), F32),
        ),
        compiler_params=_params(),
        cost_estimate=_cost(8 * 10**9, 4 * 10**6),
        name="gram_inverse",
    )(gram, up, down, before, after)


def _threshold(foldp, f):
    held = (foldp < 0.5) | ((foldp > f + 0.5) & (foldp < f + 1.5))
    return jnp.where(held, 1.0, 0.0).astype(BF)


def _fill(seen, thr, data, pred):
    thr = jnp.concatenate([thr] * (W // LANE), axis=1)
    return jnp.where(seen > thr, data, pred.astype(BF))


def _core_body(data_ref, seen_ref, l_ref, lt_ref, v_ref, out_ref):
    foldp = data_ref[:, W:].astype(F32)
    for f in range(FOLDS):
        pred = _dot_nt(l_ref[:, f * RANK : (f + 1) * RANK], v_ref[f])
        fill = _fill(seen_ref[...], _threshold(foldp, f), data_ref[:, :W], pred)
        out_ref[f] = _dot(lt_ref[f], fill)


def _core_cross(data, seen, lext, ltc, v):
    return pl.pallas_call(
        _core_body,
        out_shape=jax.ShapeDtypeStruct((FOLDS, RANK, W), F32),
        compiler_params=_params(),
        cost_estimate=_cost(3 * 10**9, 6 * 10**6),
        name="cross_core",
    )(data, seen, lext, ltc, v)


def _final_body(
    data_ref, up_ref, down_ref, before_ref, after_ref, seen_c_ref, seen_h_ref, lc_ref, lu_ref, ld_ref, lb_ref, la_ref,
    lth_ref, v_ref, cross_ref, inv_ref, got_ref, back_ref, new_ref,
):
    cat = lambda refs, cols: jnp.concatenate([r[:, cols] for r in refs], axis=0)
    halos = (up_ref, down_ref, before_ref, after_ref)
    halo = cat(halos, slice(0, W))
    foldp = cat(halos, slice(W, EXT)).astype(F32)
    lhalos = (lu_ref, ld_ref, lb_ref, la_ref)
    core_fold = data_ref[:, W:].astype(F32)
    chosen = jnp.zeros((ROWS, W), F32)
    for f in range(FOLDS):
        cols = slice(f * RANK, (f + 1) * RANK)
        pred = _dot_nt(cat(lhalos, cols), v_ref[f])
        fill = _fill(seen_h_ref[...], _threshold(foldp, f), halo, pred)
        cross = cross_ref[f] + _dot(lth_ref[f], fill)
        new = jnp.dot(inv_ref[f], cross, preferred_element_type=F32, precision=lax.Precision.HIGHEST)
        new_ref[f] = new
    lsel = []
    news = []
    for f in range(FOLDS):
        cols = slice(f * RANK, (f + 1) * RANK)
        mine = (core_fold > f + 0.5) & (core_fold < f + 1.5)
        lsel.append(jnp.where(mine, lc_ref[:, cols].astype(F32), 0.0).astype(BF))
        news.append(new_ref[f].astype(BF))
    chosen = _dot(jnp.concatenate(lsel, axis=1), jnp.concatenate(news, axis=0))
    known = jnp.concatenate([jnp.where(core_fold > 0.5, 0.0, 1.0).astype(BF)] * (W // LANE), axis=1)
    resid = (data_ref[:, :W].astype(F32) - chosen).astype(BF)
    resid = jnp.where(seen_c_ref[...] > known, resid, jnp.zeros_like(resid))
    step = 256
    for base in range(0, NSLOT, step):
        meta = got_ref[base : base + step, HALF:].astype(F32)
        m = _slot_rows((meta[:, 0:1], meta[:, 1:2], meta[:, 2:3]))
        half = ((_iota((step, 1), 0) + base) // CAP) % 2
        o = _iota((step, ROWS), 1)
        hot0 = _hot(o == jnp.where(half == 0, m, -1))
        hot1 = _hot(o == jnp.where(half == 1, m, -1))
        back = _dot(hot0, resid[:, :HALF]) + _dot(hot1, resid[:, HALF:])
        back_ref[base : base + step, :] = back.astype(BF)


def _final(data, halos, seen_c, seen_h, lext, lhalos, lth, v, cross, inv, got):
    return pl.pallas_call(
        _final_body,
        out_shape=(
            jax.ShapeDtypeStruct((NSLOT, HALF), BF),
            jax.ShapeDtypeStruct((FOLDS, RANK, W), F32),
        ),
        compiler_params=_params(),
        cost_estimate=_cost(4 * 10**9, 10**7),
        name="update_residual",
    )(data, *halos, seen_c, seen_h, lext, *lhalos, lth, v, cross, inv, got)


def _turn_body(new_ref, out_ref):
    out_ref[0] = new_ref[0].T


def _turn(new):
    return pl.pallas_call(
        _turn_body,
        grid=(FOLDS,),
        in_specs=[pl.BlockSpec((1, RANK, W), lambda f: (f, 0, 0))],
        out_specs=pl.BlockSpec((1, W, RANK), lambda f: (f, 0, 0)),
        out_shape=jax.ShapeDtypeStruct((FOLDS, W, RANK), F32),
        compiler_params=_params(),
        cost_estimate=_cost(10**6, 4 * 10**6),
        name="new_right",
    )(new)


def _return_body(ret_ref, place_ref, out_ref):
    step = 128
    for base in range(0, ROWS, step):
        place = place_ref[base : base + step, :1]
        r = _iota((step, NSLOT), 1)
        out_ref[base : base + step, :HALF] = _dot(_hot(r == place), ret_ref[...]).astype(BF)
        out_ref[base : base + step, HALF:] = _dot(_hot(r == place + CAP), ret_ref[...]).astype(BF)


def _give_back(ret, place):
    return pl.pallas_call(
        _return_body,
        out_shape=jax.ShapeDtypeStruct((ROWS, W), BF),
        compiler_params=_params(),
        cost_estimate=_cost(10**9, 4 * 10**6),
        name="give_back",
    )(ret, place)


def _swap(x):
    return lax.all_to_all(x, AXES, split_axis=0, concat_axis=0, tiled=True)


def local(acq_traces, route_owner, route_row, route_fold, sample_bits, left_factors, right_factors):
    line = lambda x: x.reshape(1, ROWS)
    send, place = _route(line(route_owner), line(route_row), line(route_fold), acq_traces)
    got = _swap(send)
    lext, *lparts = _lext(left_factors.reshape(ROWS, FOLDS * RANK), sample_bits)
    ltop, lbot, lleft, lright = lparts
    lup, ldown = _along(ltop, lbot, "mlong")
    ltc, seen_c, gram = _core_prep(lext)
    lpack = _pack(lup, ldown, lleft, lright, "margin_left")
    got, lpack, ltc, seen_c, gram = lax.optimization_barrier((got, lpack, ltc, seen_c, gram))
    data, top, bot, left, right = _place(got)
    top, bot, lpack = lax.optimization_barrier((top, bot, lpack))
    up, down = _along(top, bot, "mlong")
    lbefore, lafter = _along(*lpack, "mshort")
    pack = _pack(up, down, left, right, "margin_data")
    pack, gram = lax.optimization_barrier((pack, gram))
    halos = (up, down, *_along(*pack, "mshort"))
    lhalos = (lup, ldown, lbefore, lafter)
    cross = _core_cross(data, seen_c, lext, ltc, right_factors)
    lth, seen_h, inv = _inverse(gram, *lhalos)
    back, new = _final(data, halos, seen_c, seen_h, lext, lhalos, lth, right_factors, cross, inv, got)
    ret = _swap(back)
    new_right = _turn(new)
    return new_right, _give_back(ret, place)


def solution(mesh):
    in_specs = (
        P(AXES, None),
        P(AXES),
        P(AXES),
        P(AXES),
        P(AXES, None),
        P(AXES, None, None),
        P(None, AXES, None),
    )
    out_specs = (P(None, AXES, None), P(AXES, None))
    return jax.shard_map(local, mesh=mesh, in_specs=in_specs, out_specs=out_specs, check_vma=False)
```

```python
import functools

import jax
import jax.numpy as jnp
from jax import lax
from jax.experimental import pallas as pl
from jax.experimental.pallas import tpu as pltpu
from jax.sharding import PartitionSpec as P

RANK = 128
FOLDS = 4
H = 4
CX = 16
CY = 32
W = 1024
ROWS = CX * CY
HALF = W // 2
LANE = 128
CAP = 4
SLOT = 2 * CAP
NSLOT = 128 * SLOT
EXT = W + LANE
LEXT = FOLDS * RANK + LANE
STRIP = H * CY
SIDE = H * CX
WIDE = H * (CY + 2 * H)
HALO = 2 * SIDE + 2 * WIDE
PANEL = 16
SPLIT = 64

BF = jnp.bfloat16
F32 = jnp.float32
AXES = ("mlong", "mshort")


def _iota(shape, dim):
    return lax.broadcasted_iota(jnp.int32, shape, dim)


def _hot(cond):
    return jnp.where(cond, 1.0, 0.0).astype(BF)


def _dot(a, b):
    return jnp.dot(a, b, preferred_element_type=F32)


def _dot_nt(a, b):
    return lax.dot_general(a, b, (((1,), (1,)), ((), ())), preferred_element_type=F32)


def _params(limit=32):
    return pltpu.CompilerParams(vmem_limit_bytes=limit * 1024 * 1024)


def _cost(flops, nbytes):
    return pl.CostEstimate(flops=flops, bytes_accessed=nbytes, transcendentals=0)


_VMEM = pl.BlockSpec(memory_space=pltpu.VMEM)
_HBM = pl.BlockSpec(memory_space=pltpu.HBM)
_ANY = pl.BlockSpec(memory_space=pl.ANY)


def _weave(y):
    y = y.reshape(y.shape[0] // SLOT, SLOT, W)
    left, right = y[:, :, :HALF], y[:, :, HALF:]
    even = jnp.concatenate([left[:, :CAP], right[:, :CAP]], axis=1)
    odd = jnp.concatenate([left[:, CAP:], right[:, CAP:]], axis=1)
    return jnp.stack([even, odd], axis=1).reshape(-1, HALF)


def _side_select(shape, first):
    r = _iota(shape, 0)
    m = _iota(shape, 1)
    return _hot(m == (r // H) * CY + first + r % H)


def _route_body(
    own_hbm, row_hbm, fold_hbm, tr_hbm, send_hbm, place_ref, own_ref, row_ref, fold_ref, tr_ref, send_ref, in_sem, out_sem
):
    notes = [
        pltpu.make_async_copy(src, dst, in_sem.at[i])
        for i, (src, dst) in enumerate(((own_hbm, own_ref), (row_hbm, row_ref), (fold_hbm, fold_ref)))
    ]
    for note in notes:
        note.start()
    load = pltpu.make_async_copy(tr_hbm, tr_ref, in_sem.at[3])
    load.start()
    for note in notes:
        note.wait()
    own = own_ref[...]
    row = row_ref[...]
    valid = own >= 0
    ownf = own.astype(F32)
    sub = _iota((LANE, ROWS), 0)
    flag = jnp.where(valid, 1.0, 0.0)
    meta = jnp.where(sub == 0, flag, 0.0)
    meta = jnp.where(sub == 1, (row >> 5).astype(F32), meta)
    meta = jnp.where(sub == 2, (row & 31).astype(F32), meta)
    meta = jnp.where(sub == 3, (fold_ref[...] + 1).astype(F32), meta)
    meta = jnp.where(sub == 4, ownf, meta)
    meta_t = meta.T
    ocol = meta_t[:, 4:5]
    same = ocol == ownf
    rs = _iota((ROWS, ROWS), 0)
    cs = _iota((ROWS, ROWS), 1)
    within = jnp.sum(jnp.where(same & (rs < cs), 1.0, 0.0), axis=0, keepdims=True)
    place = jnp.where(valid, ownf * CAP + within, -64.0).astype(jnp.int32)
    within_c = jnp.sum(jnp.where(same & (cs < rs), 1.0, 0.0), axis=1, keepdims=True)
    place_c = jnp.where(ocol >= 0.0, ocol * SLOT + within_c, -64.0)
    place_ref[...] = jnp.broadcast_to(place_c, (ROWS, LANE)).astype(jnp.int32)
    meta_b = meta_t.astype(BF)
    load.wait()
    step = 128
    stores = []
    for i, base in enumerate(range(0, ROWS, step)):
        hot = _hot(_iota((step, ROWS), 0) + base == place)
        note = _dot(hot, meta_b)
        y = _weave(_dot(hot, tr_ref[...]))
        note = _weave(jnp.concatenate([note] * (W // LANE), axis=1))[:, :LANE]
        out = slice(2 * base, 2 * (base + step))
        send_ref[out, :HALF] = y.astype(BF)
        send_ref[out, HALF:] = note.astype(BF)
        store = pltpu.make_async_copy(send_ref.at[out], send_hbm.at[out], out_sem.at[i])
        store.start()
        stores.append(store)
    for store in stores:
        store.wait()


def _route(own, row, fold, traces):
    return pl.pallas_call(
        _route_body,
        in_specs=[_HBM] * 4,
        out_specs=(_HBM, _VMEM),
        out_shape=(
            pltpu.HBM((NSLOT, HALF + LANE), BF),
            jax.ShapeDtypeStruct((ROWS, LANE), jnp.int32),
        ),
        scratch_shapes=[
            pltpu.VMEM((1, ROWS), jnp.int32),
            pltpu.VMEM((1, ROWS), jnp.int32),
            pltpu.VMEM((1, ROWS), jnp.int32),
            pltpu.VMEM((ROWS, W), BF),
            pltpu.VMEM((NSLOT, HALF + LANE), BF),
            pltpu.SemaphoreType.DMA((4,)),
            pltpu.SemaphoreType.DMA((4,)),
        ],
        compiler_params=_params(60),
        cost_estimate=_cost(10**9, 4 * 10**6),
        name="route",
    )(own, row, fold, traces)


def _slot_rows(meta):
    return jnp.where(meta[0] > 0.5, meta[1] * CY + meta[2], -1.0).astype(jnp.int32)


def _place_body(got_ref, after_ref, core_ref, top_ref, bot_ref, left_ref, right_ref):
    meta = got_ref[:, HALF:].astype(F32).T
    m = _slot_rows((meta[0:1], meta[1:2], meta[2:3]))
    half = (_iota((1, NSLOT), 1) // CAP) % 2
    m0 = jnp.where(half == 0, m, -1)
    m1 = jnp.where(half == 1, m, -1)
    step = 128
    for base in range(0, ROWS, step):
        r = _iota((step, NSLOT), 0) + base
        hot0 = _hot(r == m0)
        hot1 = _hot(r == m1)
        d0 = _dot(hot0, got_ref[:, :HALF]).astype(BF)
        d1 = _dot(hot1, got_ref[:, :HALF]).astype(BF)
        f = _dot(hot0, got_ref[:, HALF:])[:, 3:4]
        f = jnp.broadcast_to(f, (step, LANE)).astype(BF)
        spots = [(core_ref, base)]
        if base == 0:
            spots.append((top_ref, 0))
        if base == ROWS - STRIP:
            spots.append((bot_ref, 0))
        for ref, at in spots:
            ref[at : at + step, :HALF] = d0
            ref[at : at + step, HALF:W] = d1
            ref[at : at + step, W:] = f
    core = core_ref[...]
    left_ref[...] = _dot(_side_select((SIDE, ROWS), 0), core).astype(BF)
    right_ref[...] = _dot(_side_select((SIDE, ROWS), CY - H), core).astype(BF)


def _place(got, after):
    return pl.pallas_call(
        _place_body,
        in_specs=[_VMEM, _ANY],
        out_shape=(
            jax.ShapeDtypeStruct((ROWS, EXT), BF),
            jax.ShapeDtypeStruct((STRIP, EXT), BF),
            jax.ShapeDtypeStruct((STRIP, EXT), BF),
            jax.ShapeDtypeStruct((SIDE, EXT), BF),
            jax.ShapeDtypeStruct((SIDE, EXT), BF),
        ),
        compiler_params=_params(),
        cost_estimate=_cost(10**9, 4 * 10**6),
        name="to_grid",
    )(got, after)


def _pack_body(cut, before_ref, after_ref, top_ref, bot_ref, token_ref, to_up_ref, to_down_ref):
    keep = _inner("mlong") if cut else (None, None)
    far = SIDE - H * H
    for at, strip, out, inner in ((0, top_ref, to_up_ref, keep[0]), (far, bot_ref, to_down_ref, keep[1])):
        edge = (lambda x: (x.astype(F32) * inner).astype(BF)) if cut else (lambda x: x)
        out[: H * H, :] = edge(before_ref[at : at + H * H, :])
        out[H * H : H * H + STRIP, :] = edge(strip[...])
        out[H * H + STRIP :, :] = edge(after_ref[at : at + H * H, :])


def _pack(before, after, top, bot, token, cut, name):
    width = top.shape[1]
    return pl.pallas_call(
        functools.partial(_pack_body, cut),
        in_specs=[_VMEM] * 4 + [_ANY],
        out_shape=(
            jax.ShapeDtypeStruct((WIDE, width), BF),
            jax.ShapeDtypeStruct((WIDE, width), BF),
        ),
        compiler_params=_params(),
        cost_estimate=_cost(10**7, 10**6),
        name=name,
    )(before, after, top, bot, token)


def _along(to_up, to_down, axis):
    n = lax.axis_size(axis)
    fwd = [(i, (i + 1) % n) for i in range(n)]
    before = lax.ppermute(to_down, axis, fwd)
    after = lax.ppermute(to_up, axis, [(j, i) for i, j in fwd])
    return before, after


def _inner(axis):
    at = lax.axis_index(axis)
    return jnp.where(at > 0, 1.0, 0.0), jnp.where(at < lax.axis_size(axis) - 1, 1.0, 0.0)


def _lext_body(left_ref, bits_ref, core_ref, top_ref, bot_ref, lside_ref, rside_ref):
    core_ref[:, : FOLDS * RANK] = left_ref[...]
    bits = bits_ref[...]
    low = (bits & 255).astype(F32)
    high = (bits >> 8).astype(F32)
    core_ref[:, FOLDS * RANK :] = jnp.concatenate([low, high], axis=1).astype(BF)
    core = core_ref[...]
    before, after = _inner("mshort")
    top_ref[...] = core[:STRIP]
    bot_ref[...] = core[ROWS - STRIP :]
    lside_ref[...] = (_dot(_side_select((SIDE, ROWS), 0), core) * before).astype(BF)
    rside_ref[...] = (_dot(_side_select((SIDE, ROWS), CY - H), core) * after).astype(BF)


def _lext(left, bits):
    return pl.pallas_call(
        _lext_body,
        out_shape=(
            jax.ShapeDtypeStruct((ROWS, LEXT), BF),
            jax.ShapeDtypeStruct((STRIP, LEXT), BF),
            jax.ShapeDtypeStruct((STRIP, LEXT), BF),
            jax.ShapeDtypeStruct((SIDE, LEXT), BF),
            jax.ShapeDtypeStruct((SIDE, LEXT), BF),
        ),
        compiler_params=_params(),
        cost_estimate=_cost(10**8, 2 * 10**6),
        name="left_rows",
    )(left, bits)


def _recip(x):
    r = pl.reciprocal(x, approx=True)
    return r * (2.0 - x * r)


def _split3(x):
    hi = x.astype(BF)
    rest = x - hi.astype(F32)
    mid = rest.astype(BF)
    return hi, mid, (rest - mid.astype(F32)).astype(BF)


def _outer6(a, b):
    ah, am, al = _split3(a)
    bh, bm, bl = _split3(b)
    left = jnp.concatenate([ah, ah, am, ah, am, al], axis=0)
    right = jnp.concatenate([bh, bm, bh, bl, bm, bh], axis=0)
    return lax.dot_general(left, right, (((0,), (0,)), ((), ())), preferred_element_type=F32)


def _eliminate(g_ref, first, last):
    lane = _iota((FOLDS, PANEL, RANK), 2)
    sub = _iota((FOLDS, PANEL, RANK), 1)
    lane8 = _iota((FOLDS, 8, RANK), 2)
    lane_all = _iota((RANK, RANK), 1)
    rep = lambda a, n: jnp.broadcast_to(a, (FOLDS, n, RANK))
    tall = lambda a: jnp.concatenate([a] * (PANEL // 8), axis=1)
    for lo in range(first, last, PANEL):
        start = g_ref[:, lo : lo + PANEL, :]
        x = start
        for k in range(0, PANEL, 4):
            c = lo + k
            c0, c1, c2, c3 = (rep(x[:, :, c + j : c + j + 1], PANEL) for j in range(4))
            group8 = (lane8 >= c) & (lane8 < c + 4)
            r0, r1, r2, r3 = (
                jnp.where(group8, jnp.where(lane8 == c + i, 1.0, 0.0), rep(x[:, k + i : k + i + 1, :], 8)) for i in range(4)
            )
            at = lambda col, i: rep(col[:, k + i : k + i + 1, :], 8)
            p00, p01, p02, p03 = at(c0, 0), at(c1, 0), at(c2, 0), at(c3, 0)
            e0 = _recip(p00)
            l10, l20, l30 = p01 * e0, p02 * e0, p03 * e0
            e1 = _recip(at(c1, 1) - l10 * p01)
            p12, p13 = at(c2, 1) - l10 * p02, at(c3, 1) - l10 * p03
            l21, l31 = p12 * e1, p13 * e1
            e2 = _recip(at(c2, 2) - l20 * p02 - l21 * p12)
            p23 = at(c3, 2) - l20 * p03 - l21 * p13
            l32 = p23 * e2
            e3 = _recip(at(c3, 3) - l30 * p03 - l31 * p13 - l32 * p23)
            r1 = r1 - l10 * r0
            r2 = r2 - l20 * r0 - l21 * r1
            r3 = r3 - l30 * r0 - l31 * r1 - l32 * r2
            w0, w1, w2, w3 = e0 * r0, e1 * r1, e2 * r2, e3 * r3
            c1 = c1 - tall(l10) * c0
            c2 = c2 - tall(l20) * c0 - tall(l21) * c1
            c3 = c3 - tall(l30) * c0 - tall(l31) * c1 - tall(l32) * c2
            x = jnp.where((lane >= c) & (lane < c + 4), 0.0, x)
            x = x - c0 * tall(w0) - c1 * tall(w1) - c2 * tall(w2) - c3 * tall(w3)
            z2 = w2 - l32 * w3
            z1 = w1 - l21 * z2 - l31 * w3
            z0 = w0 - l10 * z1 - l20 * z2 - l30 * w3
            for i, z in enumerate((z0, z1, z2, w3)):
                x = jnp.where(sub == k + i, tall(z), x)
        signed = jnp.where(lane < lo, -start, start)
        inside = (lane_all >= lo) & (lane_all < lo + PANEL)
        for f in range(FOLDS):
            g_ref[f] = jnp.where(inside, 0.0, g_ref[f]) - _outer6(signed[f], x[f])
        g_ref[:, lo : lo + PANEL, :] = x


def _unpack(rows):
    b = _iota((LANE, W), 0)
    o = _iota((LANE, W), 1)
    spread = _hot(b == (o // 16) + jnp.where(o % 16 >= 8, 64, 0))
    value = _dot(rows, spread).astype(jnp.int32)
    shift = _iota(value.shape, 1) % 8
    return ((value >> shift) & 1).astype(F32).astype(BF)


def _core_prep_body(core_ref, ltc_ref, seen_ref, gram_ref, token_ref):
    token_ref[...] = jnp.zeros_like(token_ref)
    eye = jnp.where(_iota((RANK, RANK), 0) == _iota((RANK, RANK), 1), 1.0, 0.0)
    for f in range(FOLDS):
        core = core_ref[:, f * RANK : (f + 1) * RANK]
        core_t = core.T
        ltc_ref[f] = core_t
        gram_ref[f] = _dot(core_t, core) + eye
    for base in range(0, ROWS, 128):
        seen_ref[base : base + 128, :] = _unpack(core_ref[base : base + 128, FOLDS * RANK :])


def _core_prep(core):
    return pl.pallas_call(
        _core_prep_body,
        out_shape=(
            jax.ShapeDtypeStruct((FOLDS, RANK, ROWS), BF),
            jax.ShapeDtypeStruct((ROWS, W), BF),
            jax.ShapeDtypeStruct((FOLDS, RANK, RANK), F32),
            jax.ShapeDtypeStruct((8, LANE), F32),
        ),
        compiler_params=_params(),
        cost_estimate=_cost(10**9, 2 * 10**6),
        name="core_prep",
    )(core)


def _inverse_first_body(gram_ref, before_ref, after_ref, up_ref, down_ref, v_ref, token_ref, lth_ref, seen_ref, pred_ref, part_ref):
    halos = (before_ref, after_ref, up_ref, down_ref)
    for f in range(FOLDS):
        halo = jnp.concatenate([r[:, f * RANK : (f + 1) * RANK] for r in halos], axis=0)
        halo_t = halo.T
        lth_ref[f] = halo_t
        part_ref[f] = gram_ref[f] + _dot(halo_t, halo)
        pred_ref[f] = _dot_nt(halo, v_ref[f]).astype(BF)
    at = 0
    for ref in halos:
        n = ref.shape[0]
        seen_ref[at : at + n, :] = _unpack(ref[:, FOLDS * RANK :])
        at += n
    _eliminate(part_ref, 0, SPLIT)


def _inverse_first(gram, before, after, up, down, v, token):
    return pl.pallas_call(
        _inverse_first_body,
        in_specs=[_VMEM] * 6 + [_ANY],
        out_shape=(
            jax.ShapeDtypeStruct((FOLDS, RANK, HALO), BF),
            jax.ShapeDtypeStruct((HALO, W), BF),
            jax.ShapeDtypeStruct((FOLDS, HALO, W), BF),
            jax.ShapeDtypeStruct((FOLDS, RANK, RANK), F32),
        ),
        compiler_params=_params(),
        cost_estimate=_cost(4 * 10**9, 4 * 10**6),
        name="inverse_first",
    )(gram, before, after, up, down, v, token)


def _inverse_second_body(part_ref, token_ref, inv_ref):
    inv_ref[...] = part_ref[...]
    _eliminate(inv_ref, SPLIT, RANK)


def _inverse_second(part, token):
    return pl.pallas_call(
        _inverse_second_body,
        in_specs=[_VMEM, _ANY],
        out_shape=jax.ShapeDtypeStruct((FOLDS, RANK, RANK), F32),
        compiler_params=_params(),
        cost_estimate=_cost(4 * 10**9, 10**6),
        name="inverse_second",
    )(part, token)


def _threshold(foldp, f):
    held = (foldp < 0.5) | ((foldp > f + 0.5) & (foldp < f + 1.5))
    return jnp.where(held, 1.0, 0.0).astype(BF)


def _fill(seen, thr, data, pred):
    thr = jnp.concatenate([thr] * (W // LANE), axis=1)
    return jnp.where(seen > thr, data, pred.astype(BF))


def _core_body(data_ref, seen_ref, l_ref, lt_ref, v_ref, out_ref):
    foldp = data_ref[:, W:].astype(F32)
    for f in range(FOLDS):
        pred = _dot_nt(l_ref[:, f * RANK : (f + 1) * RANK], v_ref[f])
        fill = _fill(seen_ref[...], _threshold(foldp, f), data_ref[:, :W], pred)
        out_ref[f] = _dot(lt_ref[f], fill)


def _core_cross(data, seen, lext, ltc, v):
    return pl.pallas_call(
        _core_body,
        out_shape=jax.ShapeDtypeStruct((FOLDS, RANK, W), F32),
        compiler_params=_params(),
        cost_estimate=_cost(3 * 10**9, 6 * 10**6),
        name="cross_core",
    )(data, seen, lext, ltc, v)


def _final_body(
    data_ref, before_ref, after_ref, up_ref, down_ref, seen_c_ref, seen_h_ref, lc_ref, lth_ref, pred_ref, cross_ref, inv_ref,
    got_ref, back_hbm, new_ref, back_ref, sem,
):
    cat = lambda refs, cols: jnp.concatenate([r[:, cols] for r in refs], axis=0)
    halos = (before_ref, after_ref, up_ref, down_ref)
    halo = cat(halos, slice(0, W))
    foldp = cat(halos, slice(W, EXT)).astype(F32)
    core_fold = data_ref[:, W:].astype(F32)
    for f in range(FOLDS):
        fill = _fill(seen_h_ref[...], _threshold(foldp, f), halo, pred_ref[f])
        cross = cross_ref[f] + _dot(lth_ref[f], fill)
        new_ref[f] = jnp.dot(inv_ref[f], cross, preferred_element_type=F32, precision=lax.Precision.HIGHEST)
    lsel = []
    news = []
    for f in range(FOLDS):
        cols = slice(f * RANK, (f + 1) * RANK)
        mine = (core_fold > f + 0.5) & (core_fold < f + 1.5)
        lsel.append(jnp.where(mine, lc_ref[:, cols].astype(F32), 0.0).astype(BF))
        news.append(new_ref[f].astype(BF))
    chosen = _dot(jnp.concatenate(lsel, axis=1), jnp.concatenate(news, axis=0))
    known = jnp.concatenate([jnp.where(core_fold > 0.5, 0.0, 1.0).astype(BF)] * (W // LANE), axis=1)
    resid = (data_ref[:, :W].astype(F32) - chosen).astype(BF)
    resid = jnp.where(seen_c_ref[...] > known, resid, jnp.zeros_like(resid))
    meta = got_ref[:, HALF:].astype(F32).reshape(LANE, 2, CAP, LANE)[:, 0].reshape(ROWS, LANE)
    m = _slot_rows((meta[:, 0:1], meta[:, 1:2], meta[:, 2:3]))
    step = 128
    stores = []
    for i, base in enumerate(range(0, ROWS, step)):
        hot = _hot(_iota((step, ROWS), 1) == m[base : base + step])
        out = slice(2 * base, 2 * (base + step))
        back_ref[out, :] = _weave(_dot(hot, resid)).astype(BF)
        store = pltpu.make_async_copy(back_ref.at[out], back_hbm.at[out], sem.at[i])
        store.start()
        stores.append(store)
    for store in stores:
        store.wait()


def _final(data, halos, seen_c, seen_h, lext, lth, pred, cross, inv, got):
    return pl.pallas_call(
        _final_body,
        in_specs=[_VMEM] * 13,
        out_specs=(_HBM, _VMEM),
        scratch_shapes=[pltpu.VMEM((NSLOT, HALF), BF), pltpu.SemaphoreType.DMA((4,))],
        out_shape=(
            pltpu.HBM((NSLOT, HALF), BF),
            jax.ShapeDtypeStruct((FOLDS, RANK, W), F32),
        ),
        compiler_params=_params(),
        cost_estimate=_cost(4 * 10**9, 10**7),
        name="update_residual",
    )(data, *halos, seen_c, seen_h, lext, lth, pred, cross, inv, got)


def _turn_body(new_ref, out_ref):
    out_ref[0] = new_ref[0].T


def _turn(new):
    return pl.pallas_call(
        _turn_body,
        grid=(FOLDS,),
        in_specs=[pl.BlockSpec((1, RANK, W), lambda f: (f, 0, 0))],
        out_specs=pl.BlockSpec((1, W, RANK), lambda f: (f, 0, 0)),
        out_shape=jax.ShapeDtypeStruct((FOLDS, W, RANK), F32),
        compiler_params=_params(),
        cost_estimate=_cost(10**6, 4 * 10**6),
        name="new_right",
    )(new)


def _return_body(ret_ref, place_ref, out_hbm, out_ref, sem):
    step = 128
    stores = []
    for i, base in enumerate(range(0, ROWS, step)):
        out = slice(base, base + step)
        place = place_ref[out, :1]
        r = _iota((step, NSLOT), 1)
        out_ref[out, :HALF] = _dot(_hot(r == place), ret_ref[...]).astype(BF)
        out_ref[out, HALF:] = _dot(_hot(r == place + CAP), ret_ref[...]).astype(BF)
        store = pltpu.make_async_copy(out_ref.at[out], out_hbm.at[out], sem.at[i])
        store.start()
        stores.append(store)
    for store in stores:
        store.wait()


def _give_back(ret, place):
    return pl.pallas_call(
        _return_body,
        in_specs=[_VMEM, _VMEM],
        out_specs=_HBM,
        out_shape=pltpu.HBM((ROWS, W), BF),
        scratch_shapes=[pltpu.VMEM((ROWS, W), BF), pltpu.SemaphoreType.DMA((4,))],
        compiler_params=_params(),
        cost_estimate=_cost(10**9, 4 * 10**6),
        name="give_back",
    )(ret, place)


def _swap(x):
    return lax.all_to_all(x, AXES, split_axis=0, concat_axis=0, tiled=True)


def local(acq_traces, route_owner, route_row, route_fold, sample_bits, left_factors, right_factors):
    line = lambda x: x.reshape(1, ROWS)
    send, place = _route(line(route_owner), line(route_row), line(route_fold), acq_traces)
    got = _swap(send)
    lext, ltop, lbot, lleft, lright = _lext(left_factors.reshape(ROWS, FOLDS * RANK), sample_bits)
    lbefore, lafter = _along(lleft, lright, "mshort")
    ltc, seen_c, gram, token = _core_prep(lext)
    data, top, bot, left, right = _place(got, token)
    before, after = _along(left, right, "mshort")
    lpack = _pack(lbefore, lafter, ltop, lbot, right, True, "margin_left")
    lhalos = (lbefore, lafter, *_along(*lpack, "mlong"))
    cross = _core_cross(data, seen_c, lext, ltc, right_factors)
    lth, seen_h, pred_h, part = _inverse_first(gram, *lhalos, right_factors, top)
    pack = _pack(before, after, top, bot, lpack[0], False, "margin_data")
    halos = (before, after, *_along(*pack, "mlong"))
    inv = _inverse_second(part, pack[0])
    back, new = _final(data, halos, seen_c, seen_h, lext, lth, pred_h, cross, inv, got)
    ret = _swap(back)
    new_right = _turn(new)
    return new_right, _give_back(ret, place)


def solution(mesh):
    in_specs = (
        P(AXES, None),
        P(AXES),
        P(AXES),
        P(AXES),
        P(AXES, None),
        P(AXES, None, None),
        P(None, AXES, None),
    )
    out_specs = (P(None, AXES, None), P(AXES, None))
    return jax.shard_map(local, mesh=mesh, in_specs=in_specs, out_specs=out_specs, check_vma=False)
```

```python
import functools

import jax
import jax.numpy as jnp
from jax import lax
from jax.experimental import pallas as pl
from jax.experimental.pallas import tpu as pltpu
from jax.sharding import PartitionSpec as P

RANK = 128
FOLDS = 4
H = 4
CX = 16
CY = 32
W = 1024
ROWS = CX * CY
HALF = W // 2
LANE = 128
CAP = 4
SLOT = 2 * CAP
NSLOT = 128 * SLOT
EXT = W + LANE
LEXT = FOLDS * RANK + LANE
STRIP = H * CY
SIDE = H * CX
WIDE = H * (CY + 2 * H)
HALO = 2 * SIDE + 2 * WIDE
PANEL = 16
SPLIT = 64

BF = jnp.bfloat16
F32 = jnp.float32
AXES = ("mlong", "mshort")


def _iota(shape, dim):
    return lax.broadcasted_iota(jnp.int32, shape, dim)


def _hot(cond):
    return jnp.where(cond, 1.0, 0.0).astype(BF)


def _dot(a, b):
    return jnp.dot(a, b, preferred_element_type=F32)


def _dot_nt(a, b):
    return lax.dot_general(a, b, (((1,), (1,)), ((), ())), preferred_element_type=F32)


def _params(limit=32):
    return pltpu.CompilerParams(vmem_limit_bytes=limit * 1024 * 1024)


def _cost(flops, nbytes):
    return pl.CostEstimate(flops=flops, bytes_accessed=nbytes, transcendentals=0)


_VMEM = pl.BlockSpec(memory_space=pltpu.VMEM)
_HBM = pl.BlockSpec(memory_space=pltpu.HBM)
_ANY = pl.BlockSpec(memory_space=pl.ANY)


def _weave(y):
    y = y.reshape(y.shape[0] // SLOT, SLOT, W)
    left, right = y[:, :, :HALF], y[:, :, HALF:]
    even = jnp.concatenate([left[:, :CAP], right[:, :CAP]], axis=1)
    odd = jnp.concatenate([left[:, CAP:], right[:, CAP:]], axis=1)
    return jnp.stack([even, odd], axis=1).reshape(-1, HALF)


def _unweave(x):
    t = x.reshape(x.shape[0] // (2 * SLOT), 2, SLOT, x.shape[1])
    join = lambda rows: jnp.concatenate([t[:, 0, rows], t[:, 1, rows]], axis=1).reshape(-1, x.shape[1])
    return join(slice(0, CAP)), join(slice(CAP, SLOT))


def _side_select(shape, first):
    r = _iota(shape, 0)
    m = _iota(shape, 1)
    return _hot(m == (r // H) * CY + first + r % H)


def _route_body(
    own_hbm, row_hbm, fold_hbm, tr_hbm, send_hbm, place_ref, own_ref, row_ref, fold_ref, tr_ref, send_ref, in_sem, out_sem
):
    notes = [
        pltpu.make_async_copy(src, dst, in_sem.at[i])
        for i, (src, dst) in enumerate(((own_hbm, own_ref), (row_hbm, row_ref), (fold_hbm, fold_ref)))
    ]
    for note in notes:
        note.start()
    load = pltpu.make_async_copy(tr_hbm, tr_ref, in_sem.at[3])
    load.start()
    for note in notes:
        note.wait()
    own = own_ref[...]
    row = row_ref[...]
    valid = own >= 0
    ownf = own.astype(F32)
    sub = _iota((LANE, ROWS), 0)
    flag = jnp.where(valid, 1.0, 0.0)
    meta = jnp.where(sub == 0, flag, 0.0)
    meta = jnp.where(sub == 1, (row >> 5).astype(F32), meta)
    meta = jnp.where(sub == 2, (row & 31).astype(F32), meta)
    meta = jnp.where(sub == 3, (fold_ref[...] + 1).astype(F32), meta)
    meta = jnp.where(sub == 4, ownf, meta)
    meta_t = meta.T
    ocol = meta_t[:, 4:5]
    same = ocol == ownf
    rs = _iota((ROWS, ROWS), 0)
    cs = _iota((ROWS, ROWS), 1)
    within = jnp.sum(jnp.where(same & (rs < cs), 1.0, 0.0), axis=0, keepdims=True)
    place = jnp.where(valid, ownf * CAP + within, -64.0).astype(jnp.int32)
    place_ref[...] = jnp.broadcast_to(place.astype(F32), (LANE, ROWS)).T.astype(jnp.int32)
    meta_b = meta_t.astype(BF)
    load.wait()
    step = 128
    stores = []
    for i, base in enumerate(range(0, ROWS, step)):
        hot = _hot(_iota((step, ROWS), 0) + base == place)
        note = _dot(hot, meta_b)
        y = _weave(_dot(hot, tr_ref[...]))
        note = _weave(jnp.concatenate([note] * (W // LANE), axis=1))[:, :LANE]
        out = slice(2 * base, 2 * (base + step))
        send_ref[out, :HALF] = y.astype(BF)
        send_ref[out, HALF:] = note.astype(BF)
        store = pltpu.make_async_copy(send_ref.at[out], send_hbm.at[out], out_sem.at[i])
        store.start()
        stores.append(store)
    for store in stores:
        store.wait()


def _route(own, row, fold, traces):
    return pl.pallas_call(
        _route_body,
        in_specs=[_HBM] * 4,
        out_specs=(_HBM, _VMEM),
        out_shape=(
            pltpu.HBM((NSLOT, HALF + LANE), BF),
            jax.ShapeDtypeStruct((ROWS, LANE), jnp.int32),
        ),
        scratch_shapes=[
            pltpu.VMEM((1, ROWS), jnp.int32),
            pltpu.VMEM((1, ROWS), jnp.int32),
            pltpu.VMEM((1, ROWS), jnp.int32),
            pltpu.VMEM((ROWS, W), BF),
            pltpu.VMEM((NSLOT, HALF + LANE), BF),
            pltpu.SemaphoreType.DMA((4,)),
            pltpu.SemaphoreType.DMA((4,)),
        ],
        compiler_params=_params(60),
        cost_estimate=_cost(10**9, 4 * 10**6),
        name="route",
    )(own, row, fold, traces)


def _slot_rows(meta):
    return jnp.where(meta[0] > 0.5, meta[1] * CY + meta[2], -1.0).astype(jnp.int32)


def _place_body(got_ref, after_ref, core_ref, top_ref, bot_ref, left_ref, right_ref):
    notes = _unweave(got_ref[:, HALF:].astype(F32))[0]
    meta = notes.T
    notes = notes.astype(BF)
    m = _slot_rows((meta[0:1], meta[1:2], meta[2:3]))
    traces = jnp.concatenate(_unweave(got_ref[:, :HALF].astype(F32)), axis=1).astype(BF)
    step = 128
    for base in range(0, ROWS, step):
        hot = _hot(_iota((step, ROWS), 0) + base == m)
        d = _dot(hot, traces).astype(BF)
        f = _dot(hot, notes)[:, 3:4]
        f = jnp.broadcast_to(f, (step, LANE)).astype(BF)
        spots = [(core_ref, base)]
        if base == 0:
            spots.append((top_ref, 0))
        if base == ROWS - STRIP:
            spots.append((bot_ref, 0))
        for ref, at in spots:
            ref[at : at + step, :W] = d
            ref[at : at + step, W:] = f
    core = core_ref[...]
    left_ref[...] = _dot(_side_select((SIDE, ROWS), 0), core).astype(BF)
    right_ref[...] = _dot(_side_select((SIDE, ROWS), CY - H), core).astype(BF)


def _place(got, after):
    return pl.pallas_call(
        _place_body,
        in_specs=[_VMEM, _ANY],
        out_shape=(
            jax.ShapeDtypeStruct((ROWS, EXT), BF),
            jax.ShapeDtypeStruct((STRIP, EXT), BF),
            jax.ShapeDtypeStruct((STRIP, EXT), BF),
            jax.ShapeDtypeStruct((SIDE, EXT), BF),
            jax.ShapeDtypeStruct((SIDE, EXT), BF),
        ),
        compiler_params=_params(),
        cost_estimate=_cost(10**9, 4 * 10**6),
        name="to_grid",
    )(got, after)


def _pack_body(cut, before_ref, after_ref, top_ref, bot_ref, token_ref, to_up_ref, to_down_ref):
    keep = _inner("mlong") if cut else (None, None)
    far = SIDE - H * H
    for at, strip, out, inner in ((0, top_ref, to_up_ref, keep[0]), (far, bot_ref, to_down_ref, keep[1])):
        edge = (lambda x: (x.astype(F32) * inner).astype(BF)) if cut else (lambda x: x)
        out[: H * H, :] = edge(before_ref[at : at + H * H, :])
        out[H * H : H * H + STRIP, :] = edge(strip[...])
        out[H * H + STRIP :, :] = edge(after_ref[at : at + H * H, :])


def _pack(before, after, top, bot, token, cut, name):
    width = top.shape[1]
    return pl.pallas_call(
        functools.partial(_pack_body, cut),
        in_specs=[_VMEM] * 4 + [_ANY],
        out_shape=(
            jax.ShapeDtypeStruct((WIDE, width), BF),
            jax.ShapeDtypeStruct((WIDE, width), BF),
        ),
        compiler_params=_params(),
        cost_estimate=_cost(10**7, 10**6),
        name=name,
    )(before, after, top, bot, token)


def _along(to_up, to_down, axis):
    n = lax.axis_size(axis)
    fwd = [(i, (i + 1) % n) for i in range(n)]
    before = lax.ppermute(to_down, axis, fwd)
    after = lax.ppermute(to_up, axis, [(j, i) for i, j in fwd])
    return before, after


def _inner(axis):
    at = lax.axis_index(axis)
    return jnp.where(at > 0, 1.0, 0.0), jnp.where(at < lax.axis_size(axis) - 1, 1.0, 0.0)


def _lext_body(left_ref, bits_ref, core_ref, top_ref, bot_ref, lside_ref, rside_ref):
    core_ref[:, : FOLDS * RANK] = left_ref[...]
    bits = bits_ref[...]
    low = (bits & 255).astype(F32)
    high = (bits >> 8).astype(F32)
    core_ref[:, FOLDS * RANK :] = jnp.concatenate([low, high], axis=1).astype(BF)
    core = core_ref[...]
    before, after = _inner("mshort")
    top_ref[...] = core[:STRIP]
    bot_ref[...] = core[ROWS - STRIP :]
    lside_ref[...] = (_dot(_side_select((SIDE, ROWS), 0), core) * before).astype(BF)
    rside_ref[...] = (_dot(_side_select((SIDE, ROWS), CY - H), core) * after).astype(BF)


def _lext(left, bits):
    return pl.pallas_call(
        _lext_body,
        out_shape=(
            jax.ShapeDtypeStruct((ROWS, LEXT), BF),
            jax.ShapeDtypeStruct((STRIP, LEXT), BF),
            jax.ShapeDtypeStruct((STRIP, LEXT), BF),
            jax.ShapeDtypeStruct((SIDE, LEXT), BF),
            jax.ShapeDtypeStruct((SIDE, LEXT), BF),
        ),
        compiler_params=_params(),
        cost_estimate=_cost(10**8, 2 * 10**6),
        name="left_rows",
    )(left, bits)


def _recip(x):
    r = pl.reciprocal(x, approx=True)
    return r * (2.0 - x * r)


def _split3(x):
    hi = x.astype(BF)
    rest = x - hi.astype(F32)
    mid = rest.astype(BF)
    return hi, mid, (rest - mid.astype(F32)).astype(BF)


def _outer6(a, b):
    ah, am, al = _split3(a)
    bh, bm, bl = _split3(b)
    left = jnp.concatenate([ah, ah, am, ah, am, al], axis=0)
    right = jnp.concatenate([bh, bm, bh, bl, bm, bh], axis=0)
    return lax.dot_general(left, right, (((0,), (0,)), ((), ())), preferred_element_type=F32)


def _dot6(a, b):
    ah, am, al = _split3(a)
    bh, bm, bl = _split3(b)
    left = jnp.concatenate([ah, ah, am, ah, am, al], axis=1)
    return _dot(left, jnp.concatenate([bh, bm, bh, bl, bm, bh], axis=0))


def _eliminate(g_ref, first, last):
    lane = _iota((FOLDS, PANEL, RANK), 2)
    sub = _iota((FOLDS, PANEL, RANK), 1)
    lane8 = _iota((FOLDS, 8, RANK), 2)
    lane_all = _iota((RANK, RANK), 1)
    rep = lambda a, n: jnp.broadcast_to(a, (FOLDS, n, RANK))
    tall = lambda a: jnp.concatenate([a] * (PANEL // 8), axis=1)
    for lo in range(first, last, PANEL):
        start = g_ref[:, lo : lo + PANEL, :]
        x = start
        for k in range(0, PANEL, 4):
            c = lo + k
            c0, c1, c2, c3 = (rep(x[:, :, c + j : c + j + 1], PANEL) for j in range(4))
            group8 = (lane8 >= c) & (lane8 < c + 4)
            r0, r1, r2, r3 = (
                jnp.where(group8, jnp.where(lane8 == c + i, 1.0, 0.0), rep(x[:, k + i : k + i + 1, :], 8)) for i in range(4)
            )
            at = lambda col, i: rep(col[:, k + i : k + i + 1, :], 8)
            p00, p01, p02, p03 = at(c0, 0), at(c1, 0), at(c2, 0), at(c3, 0)
            e0 = _recip(p00)
            l10, l20, l30 = p01 * e0, p02 * e0, p03 * e0
            e1 = _recip(at(c1, 1) - l10 * p01)
            p12, p13 = at(c2, 1) - l10 * p02, at(c3, 1) - l10 * p03
            l21, l31 = p12 * e1, p13 * e1
            e2 = _recip(at(c2, 2) - l20 * p02 - l21 * p12)
            p23 = at(c3, 2) - l20 * p03 - l21 * p13
            l32 = p23 * e2
            e3 = _recip(at(c3, 3) - l30 * p03 - l31 * p13 - l32 * p23)
            r1 = r1 - l10 * r0
            r2 = r2 - l20 * r0 - l21 * r1
            r3 = r3 - l30 * r0 - l31 * r1 - l32 * r2
            w0, w1, w2, w3 = e0 * r0, e1 * r1, e2 * r2, e3 * r3
            c1 = c1 - tall(l10) * c0
            c2 = c2 - tall(l20) * c0 - tall(l21) * c1
            c3 = c3 - tall(l30) * c0 - tall(l31) * c1 - tall(l32) * c2
            x = jnp.where((lane >= c) & (lane < c + 4), 0.0, x)
            x = x - c0 * tall(w0) - c1 * tall(w1) - c2 * tall(w2) - c3 * tall(w3)
            z2 = w2 - l32 * w3
            z1 = w1 - l21 * z2 - l31 * w3
            z0 = w0 - l10 * z1 - l20 * z2 - l30 * w3
            for i, z in enumerate((z0, z1, z2, w3)):
                x = jnp.where(sub == k + i, tall(z), x)
        signed = jnp.where(lane < lo, -start, start)
        inside = (lane_all >= lo) & (lane_all < lo + PANEL)
        for f in range(FOLDS):
            g_ref[f] = jnp.where(inside, 0.0, g_ref[f]) - _outer6(signed[f], x[f])
        g_ref[:, lo : lo + PANEL, :] = x


def _unpack(rows):
    b = _iota((LANE, W), 0)
    o = _iota((LANE, W), 1)
    spread = _hot(b == (o // 16) + jnp.where(o % 16 >= 8, 64, 0))
    value = _dot(rows, spread).astype(jnp.int32)
    shift = _iota(value.shape, 1) % 8
    return ((value >> shift) & 1).astype(F32).astype(BF)


def _core_prep_body(core_ref, ltc_ref, seen_ref, gram_ref, token_ref):
    token_ref[...] = jnp.zeros_like(token_ref)
    eye = jnp.where(_iota((RANK, RANK), 0) == _iota((RANK, RANK), 1), 1.0, 0.0)
    for f in range(FOLDS):
        core = core_ref[:, f * RANK : (f + 1) * RANK]
        core_t = core.T
        ltc_ref[f] = core_t
        gram_ref[f] = _dot(core_t, core) + eye
    for base in range(0, ROWS, 128):
        seen_ref[base : base + 128, :] = _unpack(core_ref[base : base + 128, FOLDS * RANK :])


def _core_prep(core):
    return pl.pallas_call(
        _core_prep_body,
        out_shape=(
            jax.ShapeDtypeStruct((FOLDS, RANK, ROWS), BF),
            jax.ShapeDtypeStruct((ROWS, W), BF),
            jax.ShapeDtypeStruct((FOLDS, RANK, RANK), F32),
            jax.ShapeDtypeStruct((8, LANE), F32),
        ),
        compiler_params=_params(),
        cost_estimate=_cost(10**9, 2 * 10**6),
        name="core_prep",
    )(core)


def _inverse_first_body(gram_ref, before_ref, after_ref, up_ref, down_ref, v_ref, token_ref, lth_ref, seen_ref, pred_ref, part_ref):
    halos = (before_ref, after_ref, up_ref, down_ref)
    for f in range(FOLDS):
        halo = jnp.concatenate([r[:, f * RANK : (f + 1) * RANK] for r in halos], axis=0)
        halo_t = halo.T
        lth_ref[f] = halo_t
        part_ref[f] = gram_ref[f] + _dot(halo_t, halo)
        pred_ref[f] = _dot_nt(halo, v_ref[f]).astype(BF)
    at = 0
    for ref in halos:
        n = ref.shape[0]
        seen_ref[at : at + n, :] = _unpack(ref[:, FOLDS * RANK :])
        at += n
    _eliminate(part_ref, 0, SPLIT)


def _inverse_first(gram, before, after, up, down, v, token):
    return pl.pallas_call(
        _inverse_first_body,
        in_specs=[_VMEM] * 6 + [_ANY],
        out_shape=(
            jax.ShapeDtypeStruct((FOLDS, RANK, HALO), BF),
            jax.ShapeDtypeStruct((HALO, W), BF),
            jax.ShapeDtypeStruct((FOLDS, HALO, W), BF),
            jax.ShapeDtypeStruct((FOLDS, RANK, RANK), F32),
        ),
        compiler_params=_params(),
        cost_estimate=_cost(4 * 10**9, 4 * 10**6),
        name="inverse_first",
    )(gram, before, after, up, down, v, token)


def _inverse_second_body(part_ref, token_ref, inv_ref):
    inv_ref[...] = part_ref[...]
    _eliminate(inv_ref, SPLIT, RANK)


def _inverse_second(part, token):
    return pl.pallas_call(
        _inverse_second_body,
        in_specs=[_VMEM, _ANY],
        out_shape=jax.ShapeDtypeStruct((FOLDS, RANK, RANK), F32),
        compiler_params=_params(),
        cost_estimate=_cost(4 * 10**9, 10**6),
        name="inverse_second",
    )(part, token)


def _threshold(foldp, f):
    held = (foldp < 0.5) | ((foldp > f + 0.5) & (foldp < f + 1.5))
    return jnp.where(held, 1.0, 0.0).astype(BF)


def _fill(seen, thr, data, pred):
    thr = jnp.concatenate([thr] * (W // LANE), axis=1)
    return jnp.where(seen > thr, data, pred.astype(BF))


def _core_body(data_ref, seen_ref, l_ref, lt_ref, v_ref, out_ref):
    foldp = data_ref[:, W:].astype(F32)
    for f in range(FOLDS):
        pred = _dot_nt(l_ref[:, f * RANK : (f + 1) * RANK], v_ref[f])
        fill = _fill(seen_ref[...], _threshold(foldp, f), data_ref[:, :W], pred)
        out_ref[f] = _dot(lt_ref[f], fill)


def _core_cross(data, seen, lext, ltc, v):
    return pl.pallas_call(
        _core_body,
        out_shape=jax.ShapeDtypeStruct((FOLDS, RANK, W), F32),
        compiler_params=_params(),
        cost_estimate=_cost(3 * 10**9, 6 * 10**6),
        name="cross_core",
    )(data, seen, lext, ltc, v)


def _final_body(
    data_ref, before_ref, after_ref, up_ref, down_ref, seen_c_ref, seen_h_ref, lc_ref, lth_ref, pred_ref, cross_ref, inv_ref,
    got_ref, back_hbm, new_ref, back_ref, sem,
):
    cat = lambda refs, cols: jnp.concatenate([r[:, cols] for r in refs], axis=0)
    halos = (before_ref, after_ref, up_ref, down_ref)
    halo = cat(halos, slice(0, W))
    foldp = cat(halos, slice(W, EXT)).astype(F32)
    core_fold = data_ref[:, W:].astype(F32)
    for f in range(FOLDS):
        fill = _fill(seen_h_ref[...], _threshold(foldp, f), halo, pred_ref[f])
        cross = cross_ref[f] + _dot(lth_ref[f], fill)
        new_ref[f] = _dot6(inv_ref[f], cross)
    lsel = []
    news = []
    for f in range(FOLDS):
        cols = slice(f * RANK, (f + 1) * RANK)
        mine = (core_fold > f + 0.5) & (core_fold < f + 1.5)
        lsel.append(jnp.where(mine, lc_ref[:, cols].astype(F32), 0.0).astype(BF))
        news.append(new_ref[f].astype(BF))
    chosen = _dot(jnp.concatenate(lsel, axis=1), jnp.concatenate(news, axis=0))
    known = jnp.concatenate([jnp.where(core_fold > 0.5, 0.0, 1.0).astype(BF)] * (W // LANE), axis=1)
    resid = (data_ref[:, :W].astype(F32) - chosen).astype(BF)
    resid = jnp.where(seen_c_ref[...] > known, resid, jnp.zeros_like(resid))
    meta = got_ref[:, HALF:].astype(F32).reshape(LANE, 2, CAP, LANE)[:, 0].reshape(ROWS, LANE)
    m = _slot_rows((meta[:, 0:1], meta[:, 1:2], meta[:, 2:3]))
    step = 128
    stores = []
    for i, base in enumerate(range(0, ROWS, step)):
        hot = _hot(_iota((step, ROWS), 1) == m[base : base + step])
        out = slice(2 * base, 2 * (base + step))
        back_ref[out, :] = _weave(_dot(hot, resid)).astype(BF)
        store = pltpu.make_async_copy(back_ref.at[out], back_hbm.at[out], sem.at[i])
        store.start()
        stores.append(store)
    for store in stores:
        store.wait()


def _final(data, halos, seen_c, seen_h, lext, lth, pred, cross, inv, got):
    return pl.pallas_call(
        _final_body,
        in_specs=[_VMEM] * 13,
        out_specs=(_HBM, _VMEM),
        scratch_shapes=[pltpu.VMEM((NSLOT, HALF), BF), pltpu.SemaphoreType.DMA((4,))],
        out_shape=(
            pltpu.HBM((NSLOT, HALF), BF),
            jax.ShapeDtypeStruct((FOLDS, RANK, W), F32),
        ),
        compiler_params=_params(),
        cost_estimate=_cost(4 * 10**9, 10**7),
        name="update_residual",
    )(data, *halos, seen_c, seen_h, lext, lth, pred, cross, inv, got)


def _turn_body(new_ref, out_ref):
    out_ref[0] = new_ref[0].T


def _turn(new):
    return pl.pallas_call(
        _turn_body,
        grid=(FOLDS,),
        in_specs=[pl.BlockSpec((1, RANK, W), lambda f: (f, 0, 0))],
        out_specs=pl.BlockSpec((1, W, RANK), lambda f: (f, 0, 0)),
        out_shape=jax.ShapeDtypeStruct((FOLDS, W, RANK), F32),
        compiler_params=_params(),
        cost_estimate=_cost(10**6, 4 * 10**6),
        name="new_right",
    )(new)


def _return_body(ret_ref, place_ref, out_hbm, out_ref, sem):
    ret = jnp.concatenate(_unweave(ret_ref[...].astype(F32)), axis=1).astype(BF)
    step = 128
    stores = []
    for i, base in enumerate(range(0, ROWS, step)):
        out = slice(base, base + step)
        out_ref[out, :] = _dot(_hot(_iota((step, ROWS), 1) == place_ref[out, :1]), ret).astype(BF)
        store = pltpu.make_async_copy(out_ref.at[out], out_hbm.at[out], sem.at[i])
        store.start()
        stores.append(store)
    for store in stores:
        store.wait()


def _give_back(ret, place):
    return pl.pallas_call(
        _return_body,
        in_specs=[_VMEM, _VMEM],
        out_specs=_HBM,
        out_shape=pltpu.HBM((ROWS, W), BF),
        scratch_shapes=[pltpu.VMEM((ROWS, W), BF), pltpu.SemaphoreType.DMA((4,))],
        compiler_params=_params(),
        cost_estimate=_cost(10**9, 4 * 10**6),
        name="give_back",
    )(ret, place)


def _swap(x):
    return lax.all_to_all(x, AXES, split_axis=0, concat_axis=0, tiled=True)


def local(acq_traces, route_owner, route_row, route_fold, sample_bits, left_factors, right_factors):
    line = lambda x: x.reshape(1, ROWS)
    send, place = _route(line(route_owner), line(route_row), line(route_fold), acq_traces)
    got = _swap(send)
    lext, ltop, lbot, lleft, lright = _lext(left_factors.reshape(ROWS, FOLDS * RANK), sample_bits)
    lbefore, lafter = _along(lleft, lright, "mshort")
    ltc, seen_c, gram, token = _core_prep(lext)
    data, top, bot, left, right = _place(got, token)
    before, after = _along(left, right, "mshort")
    lpack = _pack(lbefore, lafter, ltop, lbot, right, True, "margin_left")
    lhalos = (lbefore, lafter, *_along(*lpack, "mlong"))
    cross = _core_cross(data, seen_c, lext, ltc, right_factors)
    lth, seen_h, pred_h, part = _inverse_first(gram, *lhalos, right_factors, top)
    pack = _pack(before, after, top, bot, lpack[0], False, "margin_data")
    halos = (before, after, *_along(*pack, "mlong"))
    inv = _inverse_second(part, pack[0])
    back, new = _final(data, halos, seen_c, seen_h, lext, lth, pred_h, cross, inv, got)
    ret = _swap(back)
    new_right = _turn(new)
    return new_right, _give_back(ret, place)


def solution(mesh):
    in_specs = (
        P(AXES, None),
        P(AXES),
        P(AXES),
        P(AXES),
        P(AXES, None),
        P(AXES, None, None),
        P(None, AXES, None),
    )
    out_specs = (P(None, AXES, None), P(AXES, None))
    return jax.shard_map(local, mesh=mesh, in_specs=in_specs, out_specs=out_specs, check_vma=False)
```

```python
import functools

import jax
import jax.numpy as jnp
from jax import lax
from jax.experimental import pallas as pl
from jax.experimental.pallas import tpu as pltpu
from jax.sharding import PartitionSpec as P

RANK = 128
FOLDS = 4
H = 4
CX = 16
CY = 32
W = 1024
ROWS = CX * CY
HALF = W // 2
LANE = 128
CAP = 4
SLOT = 2 * CAP
NSLOT = 128 * SLOT
EXT = W + LANE
LEXT = FOLDS * RANK + LANE
STRIP = H * CY
SIDE = H * CX
WIDE = H * (CY + 2 * H)
HALO = 2 * SIDE + 2 * WIDE
PANEL = 16

BF = jnp.bfloat16
F32 = jnp.float32
AXES = ("mlong", "mshort")


def _iota(shape, dim):
    return lax.broadcasted_iota(jnp.int32, shape, dim)


def _hot(cond):
    return jnp.where(cond, 1.0, 0.0).astype(BF)


def _dot(a, b):
    return jnp.dot(a, b, preferred_element_type=F32)


def _dot_nt(a, b):
    return lax.dot_general(a, b, (((1,), (1,)), ((), ())), preferred_element_type=F32)


def _params(limit=32):
    return pltpu.CompilerParams(vmem_limit_bytes=limit * 1024 * 1024)


def _cost(flops, nbytes):
    return pl.CostEstimate(flops=flops, bytes_accessed=nbytes, transcendentals=0)


_VMEM = pl.BlockSpec(memory_space=pltpu.VMEM)
_HBM = pl.BlockSpec(memory_space=pltpu.HBM)
_ANY = pl.BlockSpec(memory_space=pl.ANY)


def _weave(y):
    y = y.reshape(y.shape[0] // SLOT, SLOT, W)
    left, right = y[:, :, :HALF], y[:, :, HALF:]
    even = jnp.concatenate([left[:, :CAP], right[:, :CAP]], axis=1)
    odd = jnp.concatenate([left[:, CAP:], right[:, CAP:]], axis=1)
    return jnp.stack([even, odd], axis=1).reshape(-1, HALF)


def _unweave(x):
    t = x.reshape(x.shape[0] // (2 * SLOT), 2, SLOT, x.shape[1])
    join = lambda rows: jnp.concatenate([t[:, 0, rows], t[:, 1, rows]], axis=1).reshape(-1, x.shape[1])
    return join(slice(0, CAP)), join(slice(CAP, SLOT))


def _side_select(shape, first):
    r = _iota(shape, 0)
    m = _iota(shape, 1)
    return _hot(m == (r // H) * CY + first + r % H)


def _route_body(
    own_hbm, row_hbm, fold_hbm, tr_hbm, send_hbm, place_ref, own_ref, row_ref, fold_ref, tr_ref, send_ref, in_sem, out_sem
):
    notes = [
        pltpu.make_async_copy(src, dst, in_sem.at[i])
        for i, (src, dst) in enumerate(((own_hbm, own_ref), (row_hbm, row_ref), (fold_hbm, fold_ref)))
    ]
    for note in notes:
        note.start()
    load = pltpu.make_async_copy(tr_hbm, tr_ref, in_sem.at[3])
    load.start()
    for note in notes:
        note.wait()
    own = own_ref[...]
    row = row_ref[...]
    valid = own >= 0
    ownf = own.astype(F32)
    sub = _iota((LANE, ROWS), 0)
    flag = jnp.where(valid, 1.0, 0.0)
    meta = jnp.where(sub == 0, flag, 0.0)
    meta = jnp.where(sub == 1, (row >> 5).astype(F32), meta)
    meta = jnp.where(sub == 2, (row & 31).astype(F32), meta)
    meta = jnp.where(sub == 3, (fold_ref[...] + 1).astype(F32), meta)
    meta = jnp.where(sub == 4, ownf, meta)
    meta_t = meta.T
    ocol = meta_t[:, 4:5]
    same = ocol == ownf
    rs = _iota((ROWS, ROWS), 0)
    cs = _iota((ROWS, ROWS), 1)
    within = jnp.sum(jnp.where(same & (rs < cs), 1.0, 0.0), axis=0, keepdims=True)
    place = jnp.where(valid, ownf * CAP + within, -64.0).astype(jnp.int32)
    meta_b = meta_t.astype(BF)
    load.wait()
    step = 128
    stores = []
    for i, base in enumerate(range(0, ROWS, step)):
        hot = _hot(_iota((step, ROWS), 0) + base == place)
        note = _dot(hot, meta_b)
        y = _weave(_dot(hot, tr_ref[...]))
        note = _weave(jnp.concatenate([note] * (W // LANE), axis=1))[:, :LANE]
        out = slice(2 * base, 2 * (base + step))
        send_ref[out, :HALF] = y.astype(BF)
        send_ref[out, HALF:] = note.astype(BF)
        store = pltpu.make_async_copy(send_ref.at[out], send_hbm.at[out], out_sem.at[i])
        store.start()
        stores.append(store)
    place_ref[...] = jnp.broadcast_to(place.astype(F32), (LANE, ROWS)).T.astype(jnp.int32)
    for store in stores:
        store.wait()


def _route(own, row, fold, traces):
    return pl.pallas_call(
        _route_body,
        in_specs=[_HBM] * 4,
        out_specs=(_HBM, _VMEM),
        out_shape=(
            pltpu.HBM((NSLOT, HALF + LANE), BF),
            jax.ShapeDtypeStruct((ROWS, LANE), jnp.int32),
        ),
        scratch_shapes=[
            pltpu.VMEM((1, ROWS), jnp.int32),
            pltpu.VMEM((1, ROWS), jnp.int32),
            pltpu.VMEM((1, ROWS), jnp.int32),
            pltpu.VMEM((ROWS, W), BF),
            pltpu.VMEM((NSLOT, HALF + LANE), BF),
            pltpu.SemaphoreType.DMA((4,)),
            pltpu.SemaphoreType.DMA((4,)),
        ],
        compiler_params=_params(60),
        cost_estimate=_cost(10**9, 4 * 10**6),
        name="route",
    )(own, row, fold, traces)


def _slot_rows(meta):
    return jnp.where(meta[0] > 0.5, meta[1] * CY + meta[2], -1.0).astype(jnp.int32)


def _place_body(got_ref, after_ref, core_ref, top_ref, bot_ref, left_ref, right_ref):
    notes = _unweave(got_ref[:, HALF:].astype(F32))[0]
    meta = notes.T
    notes = notes.astype(BF)
    m = _slot_rows((meta[0:1], meta[1:2], meta[2:3]))
    traces = jnp.concatenate(_unweave(got_ref[:, :HALF].astype(F32)), axis=1).astype(BF)
    step = 128
    for base in range(0, ROWS, step):
        hot = _hot(_iota((step, ROWS), 0) + base == m)
        d = _dot(hot, traces).astype(BF)
        f = _dot(hot, notes)[:, 3:4]
        f = jnp.broadcast_to(f, (step, LANE)).astype(BF)
        spots = [(core_ref, base)]
        if base == 0:
            spots.append((top_ref, 0))
        if base == ROWS - STRIP:
            spots.append((bot_ref, 0))
        for ref, at in spots:
            ref[at : at + step, :W] = d
            ref[at : at + step, W:] = f
    core = core_ref[...]
    left_ref[...] = _dot(_side_select((SIDE, ROWS), 0), core).astype(BF)
    right_ref[...] = _dot(_side_select((SIDE, ROWS), CY - H), core).astype(BF)


def _place(got, after):
    return pl.pallas_call(
        _place_body,
        in_specs=[_VMEM, _ANY],
        out_shape=(
            jax.ShapeDtypeStruct((ROWS, EXT), BF),
            jax.ShapeDtypeStruct((STRIP, EXT), BF),
            jax.ShapeDtypeStruct((STRIP, EXT), BF),
            jax.ShapeDtypeStruct((SIDE, EXT), BF),
            jax.ShapeDtypeStruct((SIDE, EXT), BF),
        ),
        compiler_params=_params(),
        cost_estimate=_cost(10**9, 4 * 10**6),
        name="to_grid",
    )(got, after)


def _pack_body(cut, before_ref, after_ref, top_ref, bot_ref, token_ref, to_up_ref, to_down_ref):
    keep = _inner("mlong") if cut else (None, None)
    far = SIDE - H * H
    for at, strip, out, inner in ((0, top_ref, to_up_ref, keep[0]), (far, bot_ref, to_down_ref, keep[1])):
        edge = (lambda x: (x.astype(F32) * inner).astype(BF)) if cut else (lambda x: x)
        out[: H * H, :] = edge(before_ref[at : at + H * H, :])
        out[H * H : H * H + STRIP, :] = edge(strip[...])
        out[H * H + STRIP :, :] = edge(after_ref[at : at + H * H, :])


def _pack(before, after, top, bot, token, cut, name):
    width = top.shape[1]
    return pl.pallas_call(
        functools.partial(_pack_body, cut),
        in_specs=[_VMEM] * 4 + [_ANY],
        out_shape=(
            jax.ShapeDtypeStruct((WIDE, width), BF),
            jax.ShapeDtypeStruct((WIDE, width), BF),
        ),
        compiler_params=_params(),
        cost_estimate=_cost(10**7, 10**6),
        name=name,
    )(before, after, top, bot, token)


def _along(to_up, to_down, axis):
    n = lax.axis_size(axis)
    fwd = [(i, (i + 1) % n) for i in range(n)]
    before = lax.ppermute(to_down, axis, fwd)
    after = lax.ppermute(to_up, axis, [(j, i) for i, j in fwd])
    return before, after


def _inner(axis):
    at = lax.axis_index(axis)
    return jnp.where(at > 0, 1.0, 0.0), jnp.where(at < lax.axis_size(axis) - 1, 1.0, 0.0)


def _lext_body(left_ref, bits_ref, core_ref, top_ref, bot_ref, lside_ref, rside_ref):
    core_ref[:, : FOLDS * RANK] = left_ref[...]
    bits = bits_ref[...]
    low = (bits & 255).astype(F32)
    high = (bits >> 8).astype(F32)
    core_ref[:, FOLDS * RANK :] = jnp.concatenate([low, high], axis=1).astype(BF)
    core = core_ref[...]
    before, after = _inner("mshort")
    top_ref[...] = core[:STRIP]
    bot_ref[...] = core[ROWS - STRIP :]
    lside_ref[...] = (_dot(_side_select((SIDE, ROWS), 0), core) * before).astype(BF)
    rside_ref[...] = (_dot(_side_select((SIDE, ROWS), CY - H), core) * after).astype(BF)


def _lext(left, bits):
    return pl.pallas_call(
        _lext_body,
        out_shape=(
            jax.ShapeDtypeStruct((ROWS, LEXT), BF),
            jax.ShapeDtypeStruct((STRIP, LEXT), BF),
            jax.ShapeDtypeStruct((STRIP, LEXT), BF),
            jax.ShapeDtypeStruct((SIDE, LEXT), BF),
            jax.ShapeDtypeStruct((SIDE, LEXT), BF),
        ),
        compiler_params=_params(),
        cost_estimate=_cost(10**8, 2 * 10**6),
        name="left_rows",
    )(left, bits)


def _recip(x):
    r = pl.reciprocal(x, approx=True)
    return r * (2.0 - x * r)


def _split3(x):
    hi = x.astype(BF)
    rest = x - hi.astype(F32)
    mid = rest.astype(BF)
    return hi, mid, (rest - mid.astype(F32)).astype(BF)


def _outer6(a, b):
    ah, am, al = _split3(a)
    bh, bm, bl = _split3(b)
    left = jnp.concatenate([ah, ah, am, ah, am, al], axis=0)
    right = jnp.concatenate([bh, bm, bh, bl, bm, bh], axis=0)
    return lax.dot_general(left, right, (((0,), (0,)), ((), ())), preferred_element_type=F32)


def _dot6(a, b):
    ah, am, al = _split3(a)
    bh, bm, bl = _split3(b)
    left = jnp.concatenate([ah, ah, am, ah, am, al], axis=1)
    return _dot(left, jnp.concatenate([bh, bm, bh, bl, bm, bh], axis=0))


def _eliminate(g_ref, first, last):
    lane = _iota((FOLDS, PANEL, RANK), 2)
    sub = _iota((FOLDS, PANEL, RANK), 1)
    lane8 = _iota((FOLDS, 8, RANK), 2)
    lane_all = _iota((RANK, RANK), 1)
    rep = lambda a, n: jnp.broadcast_to(a, (FOLDS, n, RANK))
    tall = lambda a: jnp.concatenate([a] * (PANEL // 8), axis=1)
    for lo in range(first, last, PANEL):
        start = g_ref[:, lo : lo + PANEL, :]
        x = start
        for k in range(0, PANEL, 4):
            c = lo + k
            c0, c1, c2, c3 = (rep(x[:, :, c + j : c + j + 1], PANEL) for j in range(4))
            group8 = (lane8 >= c) & (lane8 < c + 4)
            r0, r1, r2, r3 = (
                jnp.where(group8, jnp.where(lane8 == c + i, 1.0, 0.0), rep(x[:, k + i : k + i + 1, :], 8)) for i in range(4)
            )
            at = lambda col, i: rep(col[:, k + i : k + i + 1, :], 8)
            p00, p01, p02, p03 = at(c0, 0), at(c1, 0), at(c2, 0), at(c3, 0)
            e0 = _recip(p00)
            l10, l20, l30 = p01 * e0, p02 * e0, p03 * e0
            e1 = _recip(at(c1, 1) - l10 * p01)
            p12, p13 = at(c2, 1) - l10 * p02, at(c3, 1) - l10 * p03
            l21, l31 = p12 * e1, p13 * e1
            e2 = _recip(at(c2, 2) - l20 * p02 - l21 * p12)
            p23 = at(c3, 2) - l20 * p03 - l21 * p13
            l32 = p23 * e2
            e3 = _recip(at(c3, 3) - l30 * p03 - l31 * p13 - l32 * p23)
            r1 = r1 - l10 * r0
            r2 = r2 - l20 * r0 - l21 * r1
            r3 = r3 - l30 * r0 - l31 * r1 - l32 * r2
            w0, w1, w2, w3 = e0 * r0, e1 * r1, e2 * r2, e3 * r3
            c1 = c1 - tall(l10) * c0
            c2 = c2 - tall(l20) * c0 - tall(l21) * c1
            c3 = c3 - tall(l30) * c0 - tall(l31) * c1 - tall(l32) * c2
            x = jnp.where((lane >= c) & (lane < c + 4), 0.0, x)
            x = x - c0 * tall(w0) - c1 * tall(w1) - c2 * tall(w2) - c3 * tall(w3)
            z2 = w2 - l32 * w3
            z1 = w1 - l21 * z2 - l31 * w3
            z0 = w0 - l10 * z1 - l20 * z2 - l30 * w3
            for i, z in enumerate((z0, z1, z2, w3)):
                x = jnp.where(sub == k + i, tall(z), x)
        signed = jnp.where(lane < lo, -start, start)
        inside = (lane_all >= lo) & (lane_all < lo + PANEL)
        for f in range(FOLDS):
            g_ref[f] = jnp.where(inside, 0.0, g_ref[f]) - _outer6(signed[f], x[f])
        g_ref[:, lo : lo + PANEL, :] = x


def _unpack(rows):
    b = _iota((LANE, W), 0)
    o = _iota((LANE, W), 1)
    spread = _hot(b == (o // 16) + jnp.where(o % 16 >= 8, 64, 0))
    value = _dot(rows, spread).astype(jnp.int32)
    shift = _iota(value.shape, 1) % 8
    return ((value >> shift) & 1).astype(F32).astype(BF)


def _core_prep_body(core_ref, ltc_ref, seen_ref, gram_ref, token_ref):
    token_ref[...] = jnp.zeros_like(token_ref)
    eye = jnp.where(_iota((RANK, RANK), 0) == _iota((RANK, RANK), 1), 1.0, 0.0)
    for f in range(FOLDS):
        core = core_ref[:, f * RANK : (f + 1) * RANK]
        core_t = core.T
        ltc_ref[f] = core_t
        gram_ref[f] = _dot(core_t, core) + eye
    for base in range(0, ROWS, 128):
        seen_ref[base : base + 128, :] = _unpack(core_ref[base : base + 128, FOLDS * RANK :])


def _core_prep(core):
    return pl.pallas_call(
        _core_prep_body,
        out_shape=(
            jax.ShapeDtypeStruct((FOLDS, RANK, ROWS), BF),
            jax.ShapeDtypeStruct((ROWS, W), BF),
            jax.ShapeDtypeStruct((FOLDS, RANK, RANK), F32),
            jax.ShapeDtypeStruct((8, LANE), F32),
        ),
        compiler_params=_params(),
        cost_estimate=_cost(10**9, 2 * 10**6),
        name="core_prep",
    )(core)


def _inverse_body(gram_ref, before_ref, after_ref, up_ref, down_ref, v_ref, token_ref, lth_ref, seen_ref, pred_ref, inv_ref):
    halos = (before_ref, after_ref, up_ref, down_ref)
    for f in range(FOLDS):
        halo = jnp.concatenate([r[:, f * RANK : (f + 1) * RANK] for r in halos], axis=0)
        halo_t = halo.T
        lth_ref[f] = halo_t
        inv_ref[f] = gram_ref[f] + _dot(halo_t, halo)
        pred_ref[f] = _dot_nt(halo, v_ref[f]).astype(BF)
    at = 0
    for ref in halos:
        n = ref.shape[0]
        seen_ref[at : at + n, :] = _unpack(ref[:, FOLDS * RANK :])
        at += n
    _eliminate(inv_ref, 0, RANK)


def _inverse(gram, before, after, up, down, v, token):
    return pl.pallas_call(
        _inverse_body,
        in_specs=[_VMEM] * 6 + [_ANY],
        out_shape=(
            jax.ShapeDtypeStruct((FOLDS, RANK, HALO), BF),
            jax.ShapeDtypeStruct((HALO, W), BF),
            jax.ShapeDtypeStruct((FOLDS, HALO, W), BF),
            jax.ShapeDtypeStruct((FOLDS, RANK, RANK), F32),
        ),
        compiler_params=_params(),
        cost_estimate=_cost(4 * 10**9, 4 * 10**6),
        name="gram_inverse",
    )(gram, before, after, up, down, v, token)


def _threshold(foldp, f):
    held = (foldp < 0.5) | ((foldp > f + 0.5) & (foldp < f + 1.5))
    return jnp.where(held, 1.0, 0.0).astype(BF)


def _fill(seen, thr, data, pred):
    thr = jnp.concatenate([thr] * (W // LANE), axis=1)
    return jnp.where(seen > thr, data, pred.astype(BF))


def _core_body(data_ref, seen_ref, l_ref, lt_ref, v_ref, out_ref):
    foldp = data_ref[:, W:].astype(F32)
    for f in range(FOLDS):
        pred = _dot_nt(l_ref[:, f * RANK : (f + 1) * RANK], v_ref[f])
        fill = _fill(seen_ref[...], _threshold(foldp, f), data_ref[:, :W], pred)
        out_ref[f] = _dot(lt_ref[f], fill)


def _core_cross(data, seen, lext, ltc, v):
    return pl.pallas_call(
        _core_body,
        out_shape=jax.ShapeDtypeStruct((FOLDS, RANK, W), F32),
        compiler_params=_params(),
        cost_estimate=_cost(3 * 10**9, 6 * 10**6),
        name="cross_core",
    )(data, seen, lext, ltc, v)


def _final_body(
    data_ref, before_ref, after_ref, up_ref, down_ref, seen_c_ref, seen_h_ref, lc_ref, lth_ref, pred_ref, cross_ref, inv_ref,
    got_ref, back_hbm, new_ref, back_ref, sem,
):
    cat = lambda refs, cols: jnp.concatenate([r[:, cols] for r in refs], axis=0)
    halos = (before_ref, after_ref, up_ref, down_ref)
    halo = cat(halos, slice(0, W))
    foldp = cat(halos, slice(W, EXT)).astype(F32)
    core_fold = data_ref[:, W:].astype(F32)
    for f in range(FOLDS):
        fill = _fill(seen_h_ref[...], _threshold(foldp, f), halo, pred_ref[f])
        cross = cross_ref[f] + _dot(lth_ref[f], fill)
        new_ref[f] = _dot6(inv_ref[f], cross)
    lsel = []
    news = []
    for f in range(FOLDS):
        cols = slice(f * RANK, (f + 1) * RANK)
        mine = (core_fold > f + 0.5) & (core_fold < f + 1.5)
        lsel.append(jnp.where(mine, lc_ref[:, cols].astype(F32), 0.0).astype(BF))
        news.append(new_ref[f].astype(BF))
    chosen = _dot(jnp.concatenate(lsel, axis=1), jnp.concatenate(news, axis=0))
    known = jnp.concatenate([jnp.where(core_fold > 0.5, 0.0, 1.0).astype(BF)] * (W // LANE), axis=1)
    resid = (data_ref[:, :W].astype(F32) - chosen).astype(BF)
    resid = jnp.where(seen_c_ref[...] > known, resid, jnp.zeros_like(resid))
    meta = got_ref[:, HALF:].astype(F32).reshape(LANE, 2, CAP, LANE)[:, 0].reshape(ROWS, LANE)
    m = _slot_rows((meta[:, 0:1], meta[:, 1:2], meta[:, 2:3]))
    step = 128
    stores = []
    for i, base in enumerate(range(0, ROWS, step)):
        hot = _hot(_iota((step, ROWS), 1) == m[base : base + step])
        out = slice(2 * base, 2 * (base + step))
        back_ref[out, :] = _weave(_dot(hot, resid)).astype(BF)
        store = pltpu.make_async_copy(back_ref.at[out], back_hbm.at[out], sem.at[i])
        store.start()
        stores.append(store)
    for store in stores:
        store.wait()


def _final(data, halos, seen_c, seen_h, lext, lth, pred, cross, inv, got):
    return pl.pallas_call(
        _final_body,
        in_specs=[_VMEM] * 13,
        out_specs=(_HBM, _VMEM),
        scratch_shapes=[pltpu.VMEM((NSLOT, HALF), BF), pltpu.SemaphoreType.DMA((4,))],
        out_shape=(
            pltpu.HBM((NSLOT, HALF), BF),
            jax.ShapeDtypeStruct((FOLDS, RANK, W), F32),
        ),
        compiler_params=_params(),
        cost_estimate=_cost(4 * 10**9, 10**7),
        name="update_residual",
    )(data, *halos, seen_c, seen_h, lext, lth, pred, cross, inv, got)


def _turn_body(new_ref, out_ref):
    out_ref[0] = new_ref[0].T


def _turn(new):
    return pl.pallas_call(
        _turn_body,
        grid=(FOLDS,),
        in_specs=[pl.BlockSpec((1, RANK, W), lambda f: (f, 0, 0))],
        out_specs=pl.BlockSpec((1, W, RANK), lambda f: (f, 0, 0)),
        out_shape=jax.ShapeDtypeStruct((FOLDS, W, RANK), F32),
        compiler_params=_params(),
        cost_estimate=_cost(10**6, 4 * 10**6),
        name="new_right",
    )(new)


def _return_body(ret_ref, place_ref, out_hbm, out_ref, sem):
    ret = jnp.concatenate(_unweave(ret_ref[...].astype(F32)), axis=1).astype(BF)
    step = 128
    stores = []
    for i, base in enumerate(range(0, ROWS, step)):
        out = slice(base, base + step)
        out_ref[out, :] = _dot(_hot(_iota((step, ROWS), 1) == place_ref[out, :1]), ret).astype(BF)
        store = pltpu.make_async_copy(out_ref.at[out], out_hbm.at[out], sem.at[i])
        store.start()
        stores.append(store)
    for store in stores:
        store.wait()


def _give_back(ret, place):
    return pl.pallas_call(
        _return_body,
        in_specs=[_VMEM, _VMEM],
        out_specs=_HBM,
        out_shape=pltpu.HBM((ROWS, W), BF),
        scratch_shapes=[pltpu.VMEM((ROWS, W), BF), pltpu.SemaphoreType.DMA((4,))],
        compiler_params=_params(),
        cost_estimate=_cost(10**9, 4 * 10**6),
        name="give_back",
    )(ret, place)


def _swap(x):
    return lax.all_to_all(x, AXES, split_axis=0, concat_axis=0, tiled=True)


def local(acq_traces, route_owner, route_row, route_fold, sample_bits, left_factors, right_factors):
    line = lambda x: x.reshape(1, ROWS)
    send, place = _route(line(route_owner), line(route_row), line(route_fold), acq_traces)
    got = _swap(send)
    lext, ltop, lbot, lleft, lright = _lext(left_factors.reshape(ROWS, FOLDS * RANK), sample_bits)
    lbefore, lafter = _along(lleft, lright, "mshort")
    ltc, seen_c, gram, token = _core_prep(lext)
    data, top, bot, left, right = _place(got, token)
    before, after = _along(left, right, "mshort")
    lpack = _pack(lbefore, lafter, ltop, lbot, right, True, "margin_left")
    lhalos = (lbefore, lafter, *_along(*lpack, "mlong"))
    cross = _core_cross(data, seen_c, lext, ltc, right_factors)
    pack = _pack(before, after, top, bot, lpack[0], False, "margin_data")
    halos = (before, after, *_along(*pack, "mlong"))
    lth, seen_h, pred_h, inv = _inverse(gram, *lhalos, right_factors, pack[0])
    back, new = _final(data, halos, seen_c, seen_h, lext, lth, pred_h, cross, inv, got)
    ret = _swap(back)
    new_right = _turn(new)
    return new_right, _give_back(ret, place)


def solution(mesh):
    in_specs = (
        P(AXES, None),
        P(AXES),
        P(AXES),
        P(AXES),
        P(AXES, None),
        P(AXES, None, None),
        P(None, AXES, None),
    )
    out_specs = (P(None, AXES, None), P(AXES, None))
    return jax.shard_map(local, mesh=mesh, in_specs=in_specs, out_specs=out_specs, check_vma=False)
```

```python
import functools

import jax
import jax.numpy as jnp
from jax import lax
from jax.experimental import pallas as pl
from jax.experimental.pallas import tpu as pltpu
from jax.sharding import PartitionSpec as P

RANK = 128
FOLDS = 4
H = 4
CX = 16
CY = 32
W = 1024
ROWS = CX * CY
HALF = W // 2
LANE = 128
CAP = 4
SLOT = 2 * CAP
NSLOT = 128 * SLOT
EXT = W + LANE
LEXT = FOLDS * RANK + LANE
STRIP = H * CY
SIDE = H * CX
WIDE = H * (CY + 2 * H)
HALO = 2 * SIDE + 2 * WIDE
PANEL = 16
SPLIT = 64

BF = jnp.bfloat16
F32 = jnp.float32
AXES = ("mlong", "mshort")


def _iota(shape, dim):
    return lax.broadcasted_iota(jnp.int32, shape, dim)


def _hot(cond):
    return jnp.where(cond, 1.0, 0.0).astype(BF)


def _dot(a, b):
    return jnp.dot(a, b, preferred_element_type=F32)


def _dot_nt(a, b):
    return lax.dot_general(a, b, (((1,), (1,)), ((), ())), preferred_element_type=F32)


def _params(limit=20):
    return pltpu.CompilerParams(vmem_limit_bytes=limit * 1024 * 1024)


def _cost(flops, nbytes):
    return pl.CostEstimate(flops=flops, bytes_accessed=nbytes, transcendentals=0)


_VMEM = pl.BlockSpec(memory_space=pltpu.VMEM)
_HBM = pl.BlockSpec(memory_space=pltpu.HBM)
_ANY = pl.BlockSpec(memory_space=pl.ANY)


def _weave(y):
    y = y.reshape(y.shape[0] // SLOT, SLOT, W)
    left, right = y[:, :, :HALF], y[:, :, HALF:]
    even = jnp.concatenate([left[:, :CAP], right[:, :CAP]], axis=1)
    odd = jnp.concatenate([left[:, CAP:], right[:, CAP:]], axis=1)
    return jnp.stack([even, odd], axis=1).reshape(-1, HALF)


def _unweave(x):
    t = x.reshape(x.shape[0] // (2 * SLOT), 2, SLOT, x.shape[1])
    join = lambda rows: jnp.concatenate([t[:, 0, rows], t[:, 1, rows]], axis=1).reshape(-1, x.shape[1])
    return join(slice(0, CAP)), join(slice(CAP, SLOT))


def _side_select(shape, first):
    r = _iota(shape, 0)
    m = _iota(shape, 1)
    return _hot(m == (r // H) * CY + first + r % H)


def _route_body(
    own_hbm, row_hbm, fold_hbm, tr_hbm, send_hbm, place_ref, own_ref, row_ref, fold_ref, tr_ref, send_ref, in_sem, out_sem
):
    notes = [
        pltpu.make_async_copy(src, dst, in_sem.at[i])
        for i, (src, dst) in enumerate(((own_hbm, own_ref), (row_hbm, row_ref), (fold_hbm, fold_ref)))
    ]
    for note in notes:
        note.start()
    load = pltpu.make_async_copy(tr_hbm, tr_ref, in_sem.at[3])
    load.start()
    for note in notes:
        note.wait()
    own = own_ref[...]
    row = row_ref[...]
    valid = own >= 0
    ownf = own.astype(F32)
    sub = _iota((LANE, ROWS), 0)
    flag = jnp.where(valid, 1.0, 0.0)
    meta = jnp.where(sub == 0, flag, 0.0)
    meta = jnp.where(sub == 1, (row >> 5).astype(F32), meta)
    meta = jnp.where(sub == 2, (row & 31).astype(F32), meta)
    meta = jnp.where(sub == 3, (fold_ref[...] + 1).astype(F32), meta)
    meta = jnp.where(sub == 4, ownf, meta)
    meta_t = meta.T
    ocol = meta_t[:, 4:5]
    same = ocol == ownf
    rs = _iota((ROWS, ROWS), 0)
    cs = _iota((ROWS, ROWS), 1)
    within = jnp.sum(jnp.where(same & (rs < cs), 1.0, 0.0), axis=0, keepdims=True)
    place = jnp.where(valid, ownf * CAP + within, -64.0).astype(jnp.int32)
    place_ref[...] = jnp.broadcast_to(place.astype(F32), (LANE, ROWS)).T.astype(jnp.int32)
    meta_b = meta_t.astype(BF)
    load.wait()
    step = 128
    stores = []
    for i, base in enumerate(range(0, ROWS, step)):
        hot = _hot(_iota((step, ROWS), 0) + base == place)
        note = _dot(hot, meta_b)
        y = _weave(_dot(hot, tr_ref[...]))
        note = _weave(jnp.concatenate([note] * (W // LANE), axis=1))[:, :LANE]
        out = slice(2 * base, 2 * (base + step))
        send_ref[out, :HALF] = y.astype(BF)
        send_ref[out, HALF:] = note.astype(BF)
        store = pltpu.make_async_copy(send_ref.at[out], send_hbm.at[out], out_sem.at[i])
        store.start()
        stores.append(store)
    for store in stores:
        store.wait()


def _route(own, row, fold, traces):
    return pl.pallas_call(
        _route_body,
        in_specs=[_HBM] * 4,
        out_specs=(_HBM, _VMEM),
        out_shape=(
            pltpu.HBM((NSLOT, HALF + LANE), BF),
            jax.ShapeDtypeStruct((ROWS, LANE), jnp.int32),
        ),
        scratch_shapes=[
            pltpu.VMEM((1, ROWS), jnp.int32),
            pltpu.VMEM((1, ROWS), jnp.int32),
            pltpu.VMEM((1, ROWS), jnp.int32),
            pltpu.VMEM((ROWS, W), BF),
            pltpu.VMEM((NSLOT, HALF + LANE), BF),
            pltpu.SemaphoreType.DMA((4,)),
            pltpu.SemaphoreType.DMA((4,)),
        ],
        compiler_params=_params(60),
        cost_estimate=_cost(10**9, 4 * 10**6),
        name="route",
    )(own, row, fold, traces)


def _slot_rows(meta):
    return jnp.where(meta[0] > 0.5, meta[1] * CY + meta[2], -1.0).astype(jnp.int32)


def _place_body(got_ref, after_ref, core_ref, top_ref, bot_ref, left_ref, right_ref):
    notes = _unweave(got_ref[:, HALF:].astype(F32))[0]
    meta = notes.T
    notes = notes.astype(BF)
    m = _slot_rows((meta[0:1], meta[1:2], meta[2:3]))
    traces = jnp.concatenate(_unweave(got_ref[:, :HALF].astype(F32)), axis=1).astype(BF)
    step = 128
    for base in range(0, ROWS, step):
        hot = _hot(_iota((step, ROWS), 0) + base == m)
        d = _dot(hot, traces).astype(BF)
        f = _dot(hot, notes)[:, 3:4]
        f = jnp.broadcast_to(f, (step, LANE)).astype(BF)
        spots = [(core_ref, base)]
        if base == 0:
            spots.append((top_ref, 0))
        if base == ROWS - STRIP:
            spots.append((bot_ref, 0))
        for ref, at in spots:
            ref[at : at + step, :W] = d
            ref[at : at + step, W:] = f
    core = core_ref[...]
    left_ref[...] = _dot(_side_select((SIDE, ROWS), 0), core).astype(BF)
    right_ref[...] = _dot(_side_select((SIDE, ROWS), CY - H), core).astype(BF)


def _place(got, after):
    return pl.pallas_call(
        _place_body,
        in_specs=[_VMEM, _ANY],
        out_shape=(
            jax.ShapeDtypeStruct((ROWS, EXT), BF),
            jax.ShapeDtypeStruct((STRIP, EXT), BF),
            jax.ShapeDtypeStruct((STRIP, EXT), BF),
            jax.ShapeDtypeStruct((SIDE, EXT), BF),
            jax.ShapeDtypeStruct((SIDE, EXT), BF),
        ),
        compiler_params=_params(),
        cost_estimate=_cost(10**9, 4 * 10**6),
        name="to_grid",
    )(got, after)


def _pack_body(cut, before_ref, after_ref, top_ref, bot_ref, token_ref, to_up_ref, to_down_ref):
    keep = _inner("mlong") if cut else (None, None)
    far = SIDE - H * H
    for at, strip, out, inner in ((0, top_ref, to_up_ref, keep[0]), (far, bot_ref, to_down_ref, keep[1])):
        edge = (lambda x: (x.astype(F32) * inner).astype(BF)) if cut else (lambda x: x)
        out[: H * H, :] = edge(before_ref[at : at + H * H, :])
        out[H * H : H * H + STRIP, :] = edge(strip[...])
        out[H * H + STRIP :, :] = edge(after_ref[at : at + H * H, :])


def _pack(before, after, top, bot, token, cut, name):
    width = top.shape[1]
    return pl.pallas_call(
        functools.partial(_pack_body, cut),
        in_specs=[_VMEM] * 4 + [_ANY],
        out_shape=(
            jax.ShapeDtypeStruct((WIDE, width), BF),
            jax.ShapeDtypeStruct((WIDE, width), BF),
        ),
        compiler_params=_params(),
        cost_estimate=_cost(10**7, 10**6),
        name=name,
    )(before, after, top, bot, token)


def _along(to_up, to_down, axis):
    n = lax.axis_size(axis)
    fwd = [(i, (i + 1) % n) for i in range(n)]
    before = lax.ppermute(to_down, axis, fwd)
    after = lax.ppermute(to_up, axis, [(j, i) for i, j in fwd])
    return before, after


def _inner(axis):
    at = lax.axis_index(axis)
    return jnp.where(at > 0, 1.0, 0.0), jnp.where(at < lax.axis_size(axis) - 1, 1.0, 0.0)


def _lext_body(left_ref, bits_ref, core_ref, top_ref, bot_ref, lside_ref, rside_ref):
    core_ref[:, : FOLDS * RANK] = left_ref[...]
    bits = bits_ref[...]
    low = (bits & 255).astype(F32)
    high = (bits >> 8).astype(F32)
    core_ref[:, FOLDS * RANK :] = jnp.concatenate([low, high], axis=1).astype(BF)
    core = core_ref[...]
    before, after = _inner("mshort")
    top_ref[...] = core[:STRIP]
    bot_ref[...] = core[ROWS - STRIP :]
    lside_ref[...] = (_dot(_side_select((SIDE, ROWS), 0), core) * before).astype(BF)
    rside_ref[...] = (_dot(_side_select((SIDE, ROWS), CY - H), core) * after).astype(BF)


def _lext(left, bits):
    return pl.pallas_call(
        _lext_body,
        out_shape=(
            jax.ShapeDtypeStruct((ROWS, LEXT), BF),
            jax.ShapeDtypeStruct((STRIP, LEXT), BF),
            jax.ShapeDtypeStruct((STRIP, LEXT), BF),
            jax.ShapeDtypeStruct((SIDE, LEXT), BF),
            jax.ShapeDtypeStruct((SIDE, LEXT), BF),
        ),
        compiler_params=_params(),
        cost_estimate=_cost(10**8, 2 * 10**6),
        name="left_rows",
    )(left, bits)


def _recip(x):
    r = pl.reciprocal(x, approx=True)
    return r * (2.0 - x * r)


def _split3(x):
    hi = x.astype(BF)
    rest = x - hi.astype(F32)
    mid = rest.astype(BF)
    return hi, mid, (rest - mid.astype(F32)).astype(BF)


def _outer6(a, b):
    ah, am, al = _split3(a)
    bh, bm, bl = _split3(b)
    left = jnp.concatenate([ah, ah, am, ah, am, al], axis=0)
    right = jnp.concatenate([bh, bm, bh, bl, bm, bh], axis=0)
    return lax.dot_general(left, right, (((0,), (0,)), ((), ())), preferred_element_type=F32)


def _dot6(a, b):
    ah, am, al = _split3(a)
    bh, bm, bl = _split3(b)
    left = jnp.concatenate([ah, ah, am, ah, am, al], axis=1)
    return _dot(left, jnp.concatenate([bh, bm, bh, bl, bm, bh], axis=0))


def _eliminate(g_ref, first, last):
    lane = _iota((FOLDS, PANEL, RANK), 2)
    sub = _iota((FOLDS, PANEL, RANK), 1)
    lane8 = _iota((FOLDS, 8, RANK), 2)
    lane_all = _iota((RANK, RANK), 1)
    rep = lambda a, n: jnp.broadcast_to(a, (FOLDS, n, RANK))
    tall = lambda a: jnp.concatenate([a] * (PANEL // 8), axis=1)
    for lo in range(first, last, PANEL):
        start = g_ref[:, lo : lo + PANEL, :]
        x = start
        for k in range(0, PANEL, 4):
            c = lo + k
            c0, c1, c2, c3 = (rep(x[:, :, c + j : c + j + 1], PANEL) for j in range(4))
            group8 = (lane8 >= c) & (lane8 < c + 4)
            r0, r1, r2, r3 = (
                jnp.where(group8, jnp.where(lane8 == c + i, 1.0, 0.0), rep(x[:, k + i : k + i + 1, :], 8)) for i in range(4)
            )
            at = lambda col, i: rep(col[:, k + i : k + i + 1, :], 8)
            p00, p01, p02, p03 = at(c0, 0), at(c1, 0), at(c2, 0), at(c3, 0)
            e0 = _recip(p00)
            l10, l20, l30 = p01 * e0, p02 * e0, p03 * e0
            e1 = _recip(at(c1, 1) - l10 * p01)
            p12, p13 = at(c2, 1) - l10 * p02, at(c3, 1) - l10 * p03
            l21, l31 = p12 * e1, p13 * e1
            e2 = _recip(at(c2, 2) - l20 * p02 - l21 * p12)
            p23 = at(c3, 2) - l20 * p03 - l21 * p13
            l32 = p23 * e2
            e3 = _recip(at(c3, 3) - l30 * p03 - l31 * p13 - l32 * p23)
            r1 = r1 - l10 * r0
            r2 = r2 - l20 * r0 - l21 * r1
            r3 = r3 - l30 * r0 - l31 * r1 - l32 * r2
            w0, w1, w2, w3 = e0 * r0, e1 * r1, e2 * r2, e3 * r3
            c1 = c1 - tall(l10) * c0
            c2 = c2 - tall(l20) * c0 - tall(l21) * c1
            c3 = c3 - tall(l30) * c0 - tall(l31) * c1 - tall(l32) * c2
            x = jnp.where((lane >= c) & (lane < c + 4), 0.0, x)
            x = x - c0 * tall(w0) - c1 * tall(w1) - c2 * tall(w2) - c3 * tall(w3)
            z2 = w2 - l32 * w3
            z1 = w1 - l21 * z2 - l31 * w3
            z0 = w0 - l10 * z1 - l20 * z2 - l30 * w3
            for i, z in enumerate((z0, z1, z2, w3)):
                x = jnp.where(sub == k + i, tall(z), x)
        signed = jnp.where(lane < lo, -start, start)
        inside = (lane_all >= lo) & (lane_all < lo + PANEL)
        for f in range(FOLDS):
            g_ref[f] = jnp.where(inside, 0.0, g_ref[f]) - _outer6(signed[f], x[f])
        g_ref[:, lo : lo + PANEL, :] = x


def _unpack(rows):
    b = _iota((LANE, W), 0)
    o = _iota((LANE, W), 1)
    spread = _hot(b == (o // 16) + jnp.where(o % 16 >= 8, 64, 0))
    value = _dot(rows, spread).astype(jnp.int32)
    shift = _iota(value.shape, 1) % 8
    return ((value >> shift) & 1).astype(F32).astype(BF)


def _core_prep_body(core_ref, ltc_ref, seen_ref, gram_ref, token_ref):
    token_ref[...] = jnp.zeros_like(token_ref)
    eye = jnp.where(_iota((RANK, RANK), 0) == _iota((RANK, RANK), 1), 1.0, 0.0)
    for f in range(FOLDS):
        core = core_ref[:, f * RANK : (f + 1) * RANK]
        core_t = core.T
        ltc_ref[f] = core_t
        gram_ref[f] = _dot(core_t, core) + eye
    for base in range(0, ROWS, 128):
        seen_ref[base : base + 128, :] = _unpack(core_ref[base : base + 128, FOLDS * RANK :])


def _core_prep(core):
    return pl.pallas_call(
        _core_prep_body,
        out_shape=(
            jax.ShapeDtypeStruct((FOLDS, RANK, ROWS), BF),
            jax.ShapeDtypeStruct((ROWS, W), BF),
            jax.ShapeDtypeStruct((FOLDS, RANK, RANK), F32),
            jax.ShapeDtypeStruct((8, LANE), F32),
        ),
        compiler_params=_params(),
        cost_estimate=_cost(10**9, 2 * 10**6),
        name="core_prep",
    )(core)


def _inverse_first_body(gram_ref, before_ref, after_ref, up_ref, down_ref, v_ref, token_ref, lth_ref, seen_ref, pred_ref, part_ref):
    halos = (before_ref, after_ref, up_ref, down_ref)
    for f in range(FOLDS):
        halo = jnp.concatenate([r[:, f * RANK : (f + 1) * RANK] for r in halos], axis=0)
        halo_t = halo.T
        lth_ref[f] = halo_t
        part_ref[f] = gram_ref[f] + _dot(halo_t, halo)
        pred_ref[f] = _dot_nt(halo, v_ref[f]).astype(BF)
    at = 0
    for ref in halos:
        n = ref.shape[0]
        seen_ref[at : at + n, :] = _unpack(ref[:, FOLDS * RANK :])
        at += n
    _eliminate(part_ref, 0, SPLIT)


def _inverse_first(gram, before, after, up, down, v, token):
    return pl.pallas_call(
        _inverse_first_body,
        in_specs=[_VMEM] * 6 + [_ANY],
        out_shape=(
            jax.ShapeDtypeStruct((FOLDS, RANK, HALO), BF),
            jax.ShapeDtypeStruct((HALO, W), BF),
            jax.ShapeDtypeStruct((FOLDS, HALO, W), BF),
            jax.ShapeDtypeStruct((FOLDS, RANK, RANK), F32),
        ),
        compiler_params=_params(),
        cost_estimate=_cost(4 * 10**9, 4 * 10**6),
        name="inverse_first",
    )(gram, before, after, up, down, v, token)


def _inverse_second_body(part_ref, token_ref, inv_ref):
    inv_ref[...] = part_ref[...]
    _eliminate(inv_ref, SPLIT, RANK)


def _inverse_second(part, token):
    return pl.pallas_call(
        _inverse_second_body,
        in_specs=[_VMEM, _ANY],
        out_shape=jax.ShapeDtypeStruct((FOLDS, RANK, RANK), F32),
        compiler_params=_params(),
        cost_estimate=_cost(4 * 10**9, 10**6),
        name="inverse_second",
    )(part, token)


def _threshold(foldp, f):
    held = (foldp < 0.5) | ((foldp > f + 0.5) & (foldp < f + 1.5))
    return jnp.where(held, 1.0, 0.0).astype(BF)


def _fill(seen, thr, data, pred):
    thr = jnp.concatenate([thr] * (W // LANE), axis=1)
    return jnp.where(seen > thr, data, pred.astype(BF))


def _core_body(data_ref, seen_ref, l_ref, lt_ref, v_ref, out_ref):
    foldp = data_ref[:, W:].astype(F32)
    for f in range(FOLDS):
        pred = _dot_nt(l_ref[:, f * RANK : (f + 1) * RANK], v_ref[f])
        fill = _fill(seen_ref[...], _threshold(foldp, f), data_ref[:, :W], pred)
        out_ref[f] = _dot(lt_ref[f], fill)


def _core_cross(data, seen, lext, ltc, v):
    return pl.pallas_call(
        _core_body,
        out_shape=jax.ShapeDtypeStruct((FOLDS, RANK, W), F32),
        compiler_params=_params(),
        cost_estimate=_cost(3 * 10**9, 6 * 10**6),
        name="cross_core",
    )(data, seen, lext, ltc, v)


def _final_body(
    data_ref, before_ref, after_ref, up_ref, down_ref, seen_c_ref, seen_h_ref, lc_ref, lth_ref, pred_ref, cross_ref, inv_ref,
    got_ref, back_hbm, new_ref, back_ref, sem,
):
    cat = lambda refs, cols: jnp.concatenate([r[:, cols] for r in refs], axis=0)
    halos = (before_ref, after_ref, up_ref, down_ref)
    halo = cat(halos, slice(0, W))
    foldp = cat(halos, slice(W, EXT)).astype(F32)
    core_fold = data_ref[:, W:].astype(F32)
    for f in range(FOLDS):
        fill = _fill(seen_h_ref[...], _threshold(foldp, f), halo, pred_ref[f])
        cross = cross_ref[f] + _dot(lth_ref[f], fill)
        new_ref[f] = _dot6(inv_ref[f], cross)
    lsel = []
    news = []
    for f in range(FOLDS):
        cols = slice(f * RANK, (f + 1) * RANK)
        mine = (core_fold > f + 0.5) & (core_fold < f + 1.5)
        lsel.append(jnp.where(mine, lc_ref[:, cols].astype(F32), 0.0).astype(BF))
        news.append(new_ref[f].astype(BF))
    chosen = _dot(jnp.concatenate(lsel, axis=1), jnp.concatenate(news, axis=0))
    known = jnp.concatenate([jnp.where(core_fold > 0.5, 0.0, 1.0).astype(BF)] * (W // LANE), axis=1)
    resid = (data_ref[:, :W].astype(F32) - chosen).astype(BF)
    resid = jnp.where(seen_c_ref[...] > known, resid, jnp.zeros_like(resid))
    meta = got_ref[:, HALF:].astype(F32).reshape(LANE, 2, CAP, LANE)[:, 0].reshape(ROWS, LANE)
    m = _slot_rows((meta[:, 0:1], meta[:, 1:2], meta[:, 2:3]))
    step = 128
    stores = []
    for i, base in enumerate(range(0, ROWS, step)):
        hot = _hot(_iota((step, ROWS), 1) == m[base : base + step])
        out = slice(2 * base, 2 * (base + step))
        back_ref[out, :] = _weave(_dot(hot, resid)).astype(BF)
        store = pltpu.make_async_copy(back_ref.at[out], back_hbm.at[out], sem.at[i])
        store.start()
        stores.append(store)
    for store in stores:
        store.wait()


def _final(data, halos, seen_c, seen_h, lext, lth, pred, cross, inv, got):
    return pl.pallas_call(
        _final_body,
        in_specs=[_VMEM] * 13,
        out_specs=(_HBM, _VMEM),
        scratch_shapes=[pltpu.VMEM((NSLOT, HALF), BF), pltpu.SemaphoreType.DMA((4,))],
        out_shape=(
            pltpu.HBM((NSLOT, HALF), BF),
            jax.ShapeDtypeStruct((FOLDS, RANK, W), F32),
        ),
        compiler_params=_params(),
        cost_estimate=_cost(4 * 10**9, 10**7),
        name="update_residual",
    )(data, *halos, seen_c, seen_h, lext, lth, pred, cross, inv, got)


def _turn_body(new_ref, out_ref):
    out_ref[0] = new_ref[0].T


def _turn(new):
    return pl.pallas_call(
        _turn_body,
        grid=(FOLDS,),
        in_specs=[pl.BlockSpec((1, RANK, W), lambda f: (f, 0, 0))],
        out_specs=pl.BlockSpec((1, W, RANK), lambda f: (f, 0, 0)),
        out_shape=jax.ShapeDtypeStruct((FOLDS, W, RANK), F32),
        compiler_params=_params(),
        cost_estimate=_cost(10**6, 4 * 10**6),
        name="new_right",
    )(new)


def _return_body(ret_ref, place_ref, out_hbm, out_ref, sem):
    ret = jnp.concatenate(_unweave(ret_ref[...].astype(F32)), axis=1).astype(BF)
    step = 128
    stores = []
    for i, base in enumerate(range(0, ROWS, step)):
        out = slice(base, base + step)
        out_ref[out, :] = _dot(_hot(_iota((step, ROWS), 1) == place_ref[out, :1]), ret).astype(BF)
        store = pltpu.make_async_copy(out_ref.at[out], out_hbm.at[out], sem.at[i])
        store.start()
        stores.append(store)
    for store in stores:
        store.wait()


def _give_back(ret, place):
    return pl.pallas_call(
        _return_body,
        in_specs=[_VMEM, _VMEM],
        out_specs=_HBM,
        out_shape=pltpu.HBM((ROWS, W), BF),
        scratch_shapes=[pltpu.VMEM((ROWS, W), BF), pltpu.SemaphoreType.DMA((4,))],
        compiler_params=_params(),
        cost_estimate=_cost(10**9, 4 * 10**6),
        name="give_back",
    )(ret, place)


def _swap(x):
    return lax.all_to_all(x, AXES, split_axis=0, concat_axis=0, tiled=True)


def local(acq_traces, route_owner, route_row, route_fold, sample_bits, left_factors, right_factors):
    line = lambda x: x.reshape(1, ROWS)
    send, place = _route(line(route_owner), line(route_row), line(route_fold), acq_traces)
    got = _swap(send)
    lext, ltop, lbot, lleft, lright = _lext(left_factors.reshape(ROWS, FOLDS * RANK), sample_bits)
    lbefore, lafter = _along(lleft, lright, "mshort")
    ltc, seen_c, gram, token = _core_prep(lext)
    data, top, bot, left, right = _place(got, token)
    before, after = _along(left, right, "mshort")
    lpack = _pack(lbefore, lafter, ltop, lbot, right, True, "margin_left")
    lhalos = (lbefore, lafter, *_along(*lpack, "mlong"))
    cross = _core_cross(data, seen_c, lext, ltc, right_factors)
    lth, seen_h, pred_h, part = _inverse_first(gram, *lhalos, right_factors, top)
    pack = _pack(before, after, top, bot, lpack[0], False, "margin_data")
    halos = (before, after, *_along(*pack, "mlong"))
    inv = _inverse_second(part, pack[0])
    back, new = _final(data, halos, seen_c, seen_h, lext, lth, pred_h, cross, inv, got)
    ret = _swap(back)
    new_right = _turn(new)
    return new_right, _give_back(ret, place)


def solution(mesh):
    in_specs = (
        P(AXES, None),
        P(AXES),
        P(AXES),
        P(AXES),
        P(AXES, None),
        P(AXES, None, None),
        P(None, AXES, None),
    )
    out_specs = (P(None, AXES, None), P(AXES, None))
    return jax.shard_map(local, mesh=mesh, in_specs=in_specs, out_specs=out_specs, check_vma=False)
```
